32 devices in a mesh: lat: 4 (over x, core), lon: 8 (over z, y).
Axes of the slice: x: 2, y: 2, z: 4, core: 2. Of those that a mesh axis runs over, the one named last changes fastest.
Arguments:
- latent: bfloat16 [64, 128, 641], P('lat', 'lon'), may hold values from -6 to 6
- filters: bfloat16 [9, 64, 9, 33], P(None, 'lat'), may hold values from -0.59765625 to 0.59765625
- widths: int32 [64, 9], P('lat'), may hold values from 0 to 16, as said below
- mix_weight: bfloat16 [9, 641, 512], P(None, None, ('lat', 'lon')), may hold values from -0.078125 to 0.078125
- mix_bias: float32 [512], replicated, may hold values from -3 to 3
Outputs:
- convolved: bfloat16 [64, 128, 512], P('lat', 'lon')
The draws below stay inside these ranges and needn't reach their ends.
Inputs may be any that keep to these rules, and one draw needn't show every extreme that they name: widths grow toward the poles and are at most 16, reached in rows next to a pole.
All inputs are finite; a program needn't handle non-finite values.
Results may differ from the reference program's by a relative error of at most 0.0048.
Values may be sent and summed in bfloat16 or wider, within the bound.
No kernel may reach another device: no remote copies, remote signals or barrier semaphores. Data moves between devices by JAX's collectives and lax.ppermute only.
A program may use at most 64 MiB of HBM per device.

```python
import math
import jax
import jax.numpy as jnp
from jax import lax

CHANNELS = 641
OUT_CH = 512
BASES = 9
RADIUS = 4
LON_REACH = 16
LATITUDES = 64
LONGITUDES = 128


def draw_widths(key, part):
    row_indices = jnp.arange(LATITUDES, dtype=jnp.int32)[:, None]
    lat_offsets = jnp.arange(2 * RADIUS + 1, dtype=jnp.int32)[None, :] - RADIUS
    neighbour = row_indices + lat_offsets
    neighbour = jnp.where(neighbour < 0, -neighbour - 1, neighbour)
    neighbour = jnp.where(neighbour >= LATITUDES, 2 * LATITUDES - 1 - neighbour, neighbour)
    polar_gap = jnp.minimum(neighbour, LATITUDES - 1 - neighbour) + 1
    polar_gap = jnp.minimum(polar_gap, max(LATITUDES // 3, 1))
    chord_lengths = jnp.array([math.isqrt(4 * (RADIUS * RADIUS - offset_value * offset_value)) for offset_value in range(-RADIUS, RADIUS + 1)], jnp.int32)
    geometric = chord_lengths[None, :] * LATITUDES // (3 * polar_gap)
    jitter = jax.random.randint(key, (LATITUDES, 2 * RADIUS + 1), 0, 2, dtype=jnp.int32)
    return jnp.minimum(LON_REACH, geometric + jitter).astype(jnp.int32)


def level_of(stream_key, extent, shards, low, high):
    loudness, own = 1.0, jax.random.fold_in(stream_key, 6)
    for dim, blocks in shards:
        heights = jnp.exp(jax.random.uniform(jax.random.fold_in(own, dim), (blocks,), jnp.float32, low / len(shards), high / len(shards)))
        loudness = loudness * jnp.repeat(heights, extent[dim] // blocks).reshape([-1 if axis == dim else 1 for axis in range(len(extent))])
    return loudness


def centred(own_key, extent, spread, limit, split=(), kind=jnp.bfloat16):
    drawn = spread * jax.random.normal(own_key, extent, jnp.float32)
    if split:
        drawn = drawn * level_of(own_key, extent, split, -0.22, 0.18)
    return jnp.clip(drawn, -limit, limit).astype(kind)


def setup_inputs(seed: int = 0) -> dict:
    splits = jax.random.split(jax.random.key(seed), 6)
    return {
        "latent": centred(splits[0], (LATITUDES, LONGITUDES, CHANNELS), 1.0, 6.0, ((0, 4), (1, 8))),
        "filters": centred(splits[1], (BASES, LATITUDES, 2 * RADIUS + 1, 2 * LON_REACH + 1), 0.1, 0.59765625, ((1, 4),)),
        "widths": draw_widths(jax.random.fold_in(splits[5], 71), 0),
        "mix_weight": centred(splits[3], (BASES, CHANNELS, OUT_CH), (BASES * CHANNELS) ** -0.5, 0.078125, ((2, 32),)),
        "mix_bias": centred(splits[4], (OUT_CH,), 0.5, 3.0, (), jnp.float32),
    }


def extend_rows(latent):
    half_turn = LONGITUDES // 2
    upper_rim = jnp.roll(latent[:RADIUS][::-1], -half_turn, axis=1)
    lower_rim = jnp.roll(latent[-RADIUS:][::-1], -half_turn, axis=1)
    return jnp.concatenate([upper_rim, latent, lower_rim], 0)


def reference(latent, filters, widths, mix_weight, mix_bias):
    extended = extend_rows(latent)
    extended = jnp.concatenate([extended[:, -LON_REACH:], extended, extended[:, :LON_REACH]], 1)
    offsets = jnp.arange(2 * LON_REACH + 1, dtype=jnp.int32) - LON_REACH
    inside = jnp.abs(offsets)[None, None, :] <= widths[:, :, None]
    coefficients = jnp.where(inside[None], filters, jnp.zeros((), filters.dtype))
    weight_broadened = mix_weight.astype(jnp.float32)

    def one_row(row_index):
        slab_rows = lax.dynamic_slice_in_dim(extended, row_index, 2 * RADIUS + 1, 0).astype(jnp.float32)
        row_coefficient = lax.dynamic_index_in_dim(coefficients, row_index, 1, keepdims=False).astype(jnp.float32)

        def add_offset(shift_index, running_total):
            window = lax.dynamic_slice_in_dim(slab_rows, shift_index, LONGITUDES, 1)
            factor = lax.dynamic_index_in_dim(row_coefficient, shift_index, 2, keepdims=False)
            return running_total + jnp.einsum("kd,djc->kjc", factor, window, precision=lax.Precision.HIGHEST)

        summed = lax.fori_loop(0, 2 * LON_REACH + 1, add_offset,
                               jnp.zeros((BASES, LONGITUDES, CHANNELS), jnp.float32))
        features = lax.optimization_barrier(summed.astype(jnp.bfloat16)).astype(jnp.float32)
        channel_mixed_output = jnp.einsum("kjc,kco->jo", features, weight_broadened, precision=lax.Precision.HIGHEST) + mix_bias
        return jax.nn.gelu(channel_mixed_output, approximate=False).astype(jnp.bfloat16)

    return lax.map(one_row, jnp.arange(LATITUDES, dtype=jnp.int32))
```

```python
import functools

import jax
import jax.numpy as jnp
from jax import lax
from jax.experimental import pallas as pl
from jax.experimental.pallas import tpu as pltpu
from jax.sharding import PartitionSpec as P

AXES = ("lat", "lon")
LANES = 128
VMEM_BYTES = 48 * 1024 * 1024


def whole(count):
    return [pl.BlockSpec(memory_space=pltpu.VMEM)] * count


def call(kernel, outs, scratch, cost, *args):
    return pl.pallas_call(
        kernel,
        out_shape=outs,
        in_specs=whole(len(args)),
        out_specs=jax.tree.map(lambda _: pl.BlockSpec(memory_space=pltpu.VMEM), outs),
        scratch_shapes=scratch,
        compiler_params=pltpu.CompilerParams(vmem_limit_bytes=VMEM_BYTES),
        cost_estimate=pl.CostEstimate(flops=cost, bytes_accessed=2_000_000, transcendentals=0),
    )(*args)


def shape(dims, dtype=jnp.bfloat16):
    return jax.ShapeDtypeStruct(dims, dtype)


def route(move):
    lats, lons = lax.axis_size("lat"), lax.axis_size("lon")
    pairs = []
    for lat in range(lats):
        for lon in range(lons):
            to_lat, to_lon = move(lat, lon, lats, lons)
            pairs.append((lat * lons + lon, to_lat * lons + to_lon))
    return pairs


def swap(block, lat_bits, lon_bits):
    return lax.ppermute(
        block, AXES, route(lambda lat, lon, lats, lons: (lat ^ lat_bits, lon ^ lon_bits))
    )


def outer_move(lat, lon, lats, lons):
    if lat == 0 or lat == lats - 1:
        return lat, (lon + lons // 2) % lons
    return (lat - 1 if lat % 2 == 0 else lat + 1), lon


def along_move(lat, lon, lats, lons):
    return lat, (lon + 2 if lon % 2 else lon - 2) % lons


def across_move(lat, lon, lats, lons):
    return lat, (lon + 1 if lon % 2 else lon - 1) % lons


def halves_of(value, half, rest):
    low = value[..., :half]
    high = value[..., half:]
    pad = jnp.zeros(value.shape[:-1] + (2 * half - value.shape[-1],), value.dtype)
    return low, jnp.concatenate([high, pad], axis=-1) if rest else high


def split_kernel(half, w_ref, mine_ref, other_ref, pad_ref):
    odd = lax.axis_index("lon") % 2
    filled = w_ref.shape[2] - half
    pad_ref[...] = jnp.zeros_like(pad_ref)
    pad_ref[:, :, :filled] = w_ref[:, :, half:]
    low, high = w_ref[:, :, :half], pad_ref[...]
    mine_ref[...] = jnp.where(odd == 1, high, low)
    other_ref[...] = jnp.where(odd == 1, low, high)


def strip_kernel(half, x_ref, outer_ref, inner_ref, mine_ref, other_ref, rows_ref):
    lat, lon = lax.axis_index("lat"), lax.axis_index("lon")
    pole = (lat == 0) | (lat == lax.axis_size("lat") - 1)
    radius, rows = outer_ref.shape[0], x_ref.shape[0]
    channels = x_ref.shape[2]
    rows_ref[:, :, 2 * half - LANES :] = jnp.zeros_like(rows_ref[:, :, 2 * half - LANES :])
    rows_ref[radius : radius + rows, :, :channels] = x_ref[...]
    at_outer = jnp.where(lat % 2 == 0, 0, radius + rows)
    at_inner = jnp.where(lat % 2 == 0, radius + rows, 0)
    for r in range(radius):
        from_row = jnp.where(pole, radius - 1 - r, r)
        rows_ref[at_outer + r, :, :channels] = outer_ref[from_row]
        rows_ref[at_inner + r, :, :channels] = inner_ref[r]
    low, high = rows_ref[:, :, :half], rows_ref[:, :, half:]
    mine_ref[...] = jnp.where(lon % 2 == 1, high, low)
    other_ref[...] = jnp.where(lon % 2 == 1, low, high)


def band_kernel(reach, f_ref, w_ref, band_ref, row_ref):
    bases, span, rows, taps = f_ref.shape
    columns = band_ref.shape[1] // bases
    pitch = columns + taps - 1
    wide = band_ref.shape[2]
    offset = jnp.abs(lax.broadcasted_iota(jnp.int32, (rows, taps), 1) - reach)
    row_ref[...] = jnp.zeros_like(row_ref)
    for d in range(span):
        inside = offset <= w_ref[:, d : d + 1]
        for k in range(bases):
            tap = jnp.where(inside, f_ref[k, d].astype(jnp.float32), 0.0)
            row_ref[k, :, d * pitch : d * pitch + taps] = tap

    def one_row(i, _):
        for k in range(bases):
            same = jnp.broadcast_to(row_ref[k, pl.ds(i, 1), :], (columns, wide))
            band = pltpu.roll(same, 0, 1, stride=1, stride_axis=0)
            band_ref[i, k * columns : (k + 1) * columns, :] = band.astype(jnp.bfloat16)
        return 0

    lax.fori_loop(0, rows, one_row, 0)


def feature_kernel(span, band_ref, mine_ref, pair_ref, along_ref, across_ref, out_ref, slab_ref):
    odd = lax.axis_index("lon") % 2
    slab_ref[:, 1 + odd] = mine_ref[...]
    slab_ref[:, 2 - odd] = pair_ref[...]
    slab_ref[:, 3 * (1 - odd)] = along_ref[...]
    slab_ref[:, 3 * odd] = across_ref[...]
    bases, strips, rows, columns, half = out_ref.shape
    depth = span * 3 * columns

    def one_row(i, _):
        band = band_ref[i][:, :depth]
        for strip in range(strips):
            source = slab_ref[pl.ds(i, span), strip : strip + 3].reshape(depth, half)
            summed = jnp.dot(band, source, preferred_element_type=jnp.float32)
            out_ref[:, strip, i] = summed.astype(jnp.bfloat16).reshape(bases, columns, half)
        return 0

    lax.fori_loop(0, rows, one_row, 0)


def mix_kernel(masks, *refs):
    feature_ref, block_refs = refs[0], refs[1 : 1 + 2 * masks]
    keep_ref, send_ref, weight_ref = refs[1 + 2 * masks :]
    lat, lon = lax.axis_index("lat"), lax.axis_index("lon")
    odd = lon % 2
    bases, strips, points, half = feature_ref.shape
    for core in range(2):
        for mask in range(masks):
            place = (lat % 2 ^ core) * masks + ((lon // 2) ^ mask)
            weight_ref[:, place] = block_refs[core * masks + mask][...]
    wide = keep_ref.shape[1]

    def strip_sum(strip):
        total = jnp.zeros((points, wide), jnp.float32)
        for k in range(bases):
            total += lax.dot_general(
                feature_ref[k, strip],
                weight_ref[k].reshape(wide, half),
                (((1,), (1,)), ((), ())),
                preferred_element_type=jnp.float32,
            )
        return total

    send_ref[...] = strip_sum(1 - odd).astype(send_ref.dtype)
    keep_ref[...] = strip_sum(odd)


def body(latent, filters, widths, mix_weight, mix_bias):
    lats, lons = lax.axis_size("lat"), lax.axis_size("lon")
    lat, lon = lax.axis_index("lat"), lax.axis_index("lon")
    rows, columns, channels = latent.shape
    bases, _, span, taps = filters.shape
    radius, reach = span // 2, taps // 2
    assert reach == columns and lats % 2 == 0 and lons % 2 == 0
    half = -(-channels // (2 * LANES)) * LANES
    out_columns = mix_bias.shape[0]
    share = mix_weight.shape[2]

    even = lat % 2 == 0
    outer = lax.ppermute(
        jnp.where(even, latent[:radius], latent[-radius:]), AXES, route(outer_move)
    )
    inner = swap(jnp.where(even, latent[-radius:], latent[:radius]), 1, 0)

    weight = jnp.transpose(mix_weight, (0, 2, 1))
    halves = shape((bases, share, half))
    own_weight, pair_weight = call(
        functools.partial(split_kernel, half),
        (halves, halves),
        [pltpu.VMEM((bases, share, half), jnp.bfloat16)],
        100_000,
        weight,
    )
    got_weight = swap(pair_weight, 0, 1)
    odd = lon % 2 == 1
    first = jnp.concatenate(
        [jnp.where(odd, got_weight, own_weight), jnp.where(odd, own_weight, got_weight)], axis=1
    )

    strip = shape((rows + 2 * radius, columns, half))
    mine, other = call(
        functools.partial(strip_kernel, half),
        (strip, strip),
        [pltpu.VMEM((rows + 2 * radius, columns, 2 * half), jnp.bfloat16)],
        100_000,
        latent,
        outer,
        inner,
    )
    pair_strip = swap(other, 0, 1)
    along = lax.ppermute(mine, AXES, route(along_move))
    across = lax.ppermute(other, AXES, route(across_move))

    lon_masks, lat_masks = lons // 2, lats // 2
    blocks = {(0, 0): first}
    bit = lon_masks // 2
    while bit:
        for low, mask in list(blocks):
            blocks[low, mask ^ bit] = swap(blocks[low, mask], 0, 2 * bit)
        bit //= 2
    bit = 1
    while bit < lat_masks:
        for low, mask in list(blocks):
            blocks[low ^ bit, mask] = swap(blocks[low, mask], 2 * bit, 0)
        bit *= 2
    crossed = {key: swap(block, 1, 0) for key, block in blocks.items()}

    depth = span * (columns + taps - 1)
    deep = -(-depth // LANES) * LANES
    band = call(
        functools.partial(band_kernel, reach),
        shape((rows, bases * columns, deep)),
        [pltpu.VMEM((bases, rows, deep), jnp.float32)],
        1_000_000_000,
        jnp.transpose(filters, (0, 2, 1, 3)),
        widths,
    )
    features = call(
        functools.partial(feature_kernel, span),
        shape((bases, 2, rows, columns, half)),
        [pltpu.VMEM((rows + 2 * radius, 4, columns, half), jnp.bfloat16)],
        4_000_000_000,
        band,
        mine,
        pair_strip,
        along,
        across,
    ).reshape(bases, 2, rows * columns, half)

    width = out_columns // lat_masks
    pieces = []
    for low in range(lat_masks):
        operands = [blocks[low, mask] for mask in range(lon_masks)]
        operands += [crossed[low, mask] for mask in range(lon_masks)]
        keep, send = call(
            functools.partial(mix_kernel, lon_masks),
            (shape((rows * columns, width), jnp.float32), shape((rows * columns, width))),
            [pltpu.VMEM((bases, 2 * lon_masks, 2 * share, half), jnp.bfloat16)],
            2_000_000_000,
            features,
            *operands,
        )
        pieces.append(keep + swap(send, 0, 1).astype(jnp.float32))
    mixed = jnp.stack(pieces, 1)
    order = jnp.arange(lat_masks) ^ (lat // 2)
    if lat_masks == 2:
        mixed = jnp.where(lat // 2 == 0, mixed, mixed[:, ::-1])
    else:
        mixed = jnp.take(mixed, order, axis=1)
    mixed = mixed.reshape(rows, columns, out_columns) + mix_bias
    return jax.nn.gelu(mixed, approximate=False).astype(jnp.bfloat16)


def solution(mesh):
    placed = (
        P("lat", "lon", None),
        P(None, "lat", None, None),
        P("lat", None),
        P(None, None, ("lat", "lon")),
        P(),
    )
    return jax.shard_map(
        body, mesh=mesh, in_specs=placed, out_specs=P("lat", "lon", None), check_vma=False
    )
```

```python
import functools

import jax
import jax.numpy as jnp
from jax import lax
from jax.experimental import pallas as pl
from jax.experimental.pallas import tpu as pltpu
from jax.sharding import PartitionSpec as P

AXES = ("lat", "lon")
LANES = 128
VMEM_BYTES = 20 * 1024 * 1024


def call(kernel, outs, scratch, cost, *args, after=(), place=pltpu.VMEM):
    held = pl.BlockSpec(memory_space=pltpu.VMEM)
    count = len(args)

    def ordered(*refs):
        kernel(*refs[:count], *refs[count + len(after) :])

    return pl.pallas_call(
        ordered,
        out_shape=outs,
        in_specs=[pl.BlockSpec(memory_space=place)] * count + [pl.BlockSpec(memory_space=pl.ANY)] * len(after),
        out_specs=jax.tree.map(lambda _: held, outs),
        scratch_shapes=scratch,
        compiler_params=pltpu.CompilerParams(vmem_limit_bytes=VMEM_BYTES),
        cost_estimate=pl.CostEstimate(flops=cost, bytes_accessed=2_000_000, transcendentals=0),
    )(*args, *after)


def shape(dims, dtype=jnp.bfloat16):
    return jax.ShapeDtypeStruct(dims, dtype)


def route(move):
    lats, lons = lax.axis_size("lat"), lax.axis_size("lon")
    pairs = []
    for lat in range(lats):
        for lon in range(lons):
            to_lat, to_lon = move(lat, lon, lats, lons)
            pairs.append((lat * lons + lon, to_lat * lons + to_lon))
    return pairs


def swap(block, lat_bits, lon_bits):
    return lax.ppermute(
        block, AXES, route(lambda lat, lon, lats, lons: (lat ^ lat_bits, lon ^ lon_bits))
    )


def outer_move(lat, lon, lats, lons):
    if lat == 0 or lat == lats - 1:
        return lat, (lon + lons // 2) % lons
    return (lat - 1 if lat % 2 == 0 else lat + 1), lon


def along_move(lat, lon, lats, lons):
    return lat, (lon + 2 if lon % 2 else lon - 2) % lons


def across_move(lat, lon, lats, lons):
    return lat, (lon + 1 if lon % 2 else lon - 1) % lons


def start_kernel(w_hbm, x_hbm, f_hbm, own_ref, pair_ref, outer_ref, inner_ref, x_ref, f_ref, w_ref, sems):
    copies = [
        pltpu.make_async_copy(source, target, sems.at[at])
        for at, (source, target) in enumerate([(w_hbm, w_ref), (x_hbm, x_ref), (f_hbm, f_ref)])
    ]
    for copy in copies:
        copy.start()
    copies[0].wait()
    odd = lax.axis_index("lon") % 2
    half = own_ref.shape[2]
    filled = w_ref.shape[2] - half
    low, high = w_ref[:, :, :half], w_ref[:, :, half:]
    own_ref[...] = jnp.zeros_like(own_ref)
    pair_ref[...] = jnp.zeros_like(pair_ref)

    @pl.when(odd == 0)
    def _():
        own_ref[...] = low
        pair_ref[:, :, :filled] = high

    @pl.when(odd == 1)
    def _():
        own_ref[:, :, :filled] = high
        pair_ref[...] = low

    copies[1].wait()
    radius = outer_ref.shape[0]
    odd = lax.axis_index("lat") % 2
    low, high = x_ref[:radius], x_ref[-radius:]
    outer_ref[...] = jnp.where(odd == 1, high, low)
    inner_ref[...] = jnp.where(odd == 1, low, high)
    copies[2].wait()


def join_kernel(mine_ref, other_ref, out_ref):
    odd = lax.axis_index("lon") % 2
    share = mine_ref.shape[1]
    low, high = mine_ref[...], other_ref[...]
    out_ref[:, :share] = jnp.where(odd == 1, high, low)
    out_ref[:, share:] = jnp.where(odd == 1, low, high)


def stack_kernel(*refs):
    for at, ref in enumerate(refs[:-1]):
        refs[-1][at] = ref[...]


def strip_kernel(half, x_ref, outer_ref, inner_ref, mine_ref, other_ref, rows_ref):
    lat, lon = lax.axis_index("lat"), lax.axis_index("lon")
    pole = (lat == 0) | (lat == lax.axis_size("lat") - 1)
    radius, rows = outer_ref.shape[0], x_ref.shape[0]
    channels = x_ref.shape[2]
    rows_ref[:, :, 2 * half - LANES :] = jnp.zeros_like(rows_ref[:, :, 2 * half - LANES :])
    rows_ref[radius : radius + rows, :, :channels] = x_ref[...]
    at_outer = jnp.where(lat % 2 == 0, 0, radius + rows)
    at_inner = jnp.where(lat % 2 == 0, radius + rows, 0)
    for r in range(radius):
        from_row = jnp.where(pole, radius - 1 - r, r)
        rows_ref[at_outer + r, :, :channels] = outer_ref[from_row]
        rows_ref[at_inner + r, :, :channels] = inner_ref[r]
    low, high = rows_ref[:, :, :half], rows_ref[:, :, half:]
    mine_ref[...] = jnp.where(lon % 2 == 1, high, low)
    other_ref[...] = jnp.where(lon % 2 == 1, low, high)


def band_kernel(reach, f_ref, w_ref, band_ref, row_ref):
    bases, span, rows, taps = f_ref.shape
    columns = band_ref.shape[1] // (2 * bases)
    pitch = columns + taps - 1
    wide = band_ref.shape[2]
    offset = jnp.abs(lax.broadcasted_iota(jnp.int32, (rows, taps), 1) - reach)
    row_ref[...] = jnp.zeros_like(row_ref)
    for d in range(span):
        inside = offset <= w_ref[:, d : d + 1]
        for k in range(bases):
            tap = jnp.where(inside, f_ref[k, d].astype(jnp.float32), 0.0)
            row_ref[k, :, d * pitch : d * pitch + taps] = tap

    def one_pair(pair, _):
        for e in range(2):
            for k in range(bases):
                same = jnp.broadcast_to(row_ref[k, pl.ds(2 * pair + e, 1), :], (columns, wide))
                band = pltpu.roll(same, e * pitch, 1, stride=1, stride_axis=0)
                at = (e * bases + k) * columns
                band_ref[pair, at : at + columns, :] = band.astype(jnp.bfloat16)
        return 0

    lax.fori_loop(0, rows // 2, one_pair, 0)


def feature_kernel(span, band_ref, mine_ref, pair_ref, along_ref, across_ref, out_ref, slab_ref):
    odd = lax.axis_index("lon") % 2
    slab_ref[:, 1 + odd] = mine_ref[...]
    slab_ref[:, 2 - odd] = pair_ref[...]
    slab_ref[:, 3 * (1 - odd)] = along_ref[...]
    slab_ref[:, 3 * odd] = across_ref[...]
    bases, strips, rows, columns, half = out_ref.shape
    depth = (span + 1) * 3 * columns

    def one_pair(pair, _):
        band = band_ref[pair][:, :depth]
        source = [
            slab_ref[pl.ds(2 * pair, span + 1), strip : strip + 3].reshape(depth, half)
            for strip in range(strips)
        ]
        summed = jnp.dot(
            band, jnp.concatenate(source, axis=1), preferred_element_type=jnp.float32
        ).astype(jnp.bfloat16)
        for e in range(2):
            for strip in range(strips):
                part = summed[e * bases * columns : (e + 1) * bases * columns]
                part = part[:, strip * half : (strip + 1) * half]
                out_ref[:, strip, 2 * pair + e] = part.reshape(bases, columns, half)
        return 0

    lax.fori_loop(0, rows // 2, one_pair, 0)


def mix_kernel(sources, feature_ref, *refs):
    piece_refs = refs[: len(sources)]
    keep_ref, send_ref, weight_ref = refs[len(sources) :]
    lat, lon = lax.axis_index("lat"), lax.axis_index("lon")
    odd = lon % 2
    bases, strips, points, half = feature_ref.shape
    masks = weight_ref.shape[1] // 2
    for (core, held), ref in zip(sources, piece_refs):
        for at, mask in enumerate(held):
            place = (lat % 2 ^ core) * masks + ((lon // 2) ^ mask)
            weight_ref[:, place] = ref[at]
    wide = keep_ref.shape[1]

    def strip_sum(strip):
        total = jnp.zeros((points, wide), jnp.float32)
        for k in range(bases):
            total += lax.dot_general(
                feature_ref[k, strip],
                weight_ref[k].reshape(wide, half),
                (((1,), (1,)), ((), ())),
                preferred_element_type=jnp.float32,
            )
        return total

    send_ref[...] = strip_sum(1 - odd).astype(send_ref.dtype)
    keep_ref[...] = strip_sum(odd)


def finish_kernel(count, *refs):
    bias_ref, out_ref = refs[2 * count :]
    share = lax.axis_index("lat") // 2
    for low in range(count):
        keep_ref, got_ref = refs[2 * low : 2 * low + 2]
        wide = keep_ref.shape[1]
        at = pl.ds(pl.multiple_of((share ^ low) * wide, LANES), wide)
        total = keep_ref[...] + got_ref[...].astype(jnp.float32) + bias_ref[:, at]
        grown = 0.5 * total * (1.0 + lax.erf(total * 0.5**0.5))
        out_ref[:, at] = grown.astype(out_ref.dtype)


def body(latent, filters, widths, mix_weight, mix_bias):
    lats, lons = lax.axis_size("lat"), lax.axis_size("lon")
    rows, columns, channels = latent.shape
    bases, _, span, taps = filters.shape
    radius, reach = span // 2, taps // 2
    assert reach == columns and rows % 2 == lats % 2 == lons % 2 == 0
    half = -(-channels // (2 * LANES)) * LANES
    out_columns, share = mix_bias.shape[0], mix_weight.shape[2]

    edge, halves = shape((radius, columns, channels)), shape((bases, share, half))
    weights = jnp.transpose(mix_weight, (0, 2, 1))
    taps_first = jnp.transpose(filters, (0, 2, 1, 3))
    own_weight, pair_weight, outer, inner, held_latent, held_filters = call(
        start_kernel,
        (halves, halves, edge, edge, shape(latent.shape), shape(taps_first.shape)),
        [pltpu.VMEM(weights.shape, jnp.bfloat16), pltpu.SemaphoreType.DMA((3,))],
        100_000,
        weights,
        latent,
        taps_first,
        place=pltpu.HBM,
    )
    got_weight = swap(pair_weight, 0, 1)
    from_outer = lax.ppermute(outer, AXES, route(outer_move))
    from_inner = swap(inner, 1, 0)
    block = shape((bases, 2 * share, half))
    first = call(
        join_kernel, block, [], 100_000, own_weight, got_weight, after=(from_outer, from_inner)
    )

    strip = shape((rows + 2 * radius, columns, half))
    mine, other = call(
        functools.partial(strip_kernel, half),
        (strip, strip),
        [pltpu.VMEM((rows + 2 * radius, columns, 2 * half), jnp.bfloat16)],
        100_000,
        held_latent,
        from_outer,
        from_inner,
        after=(first,),
    )
    pair_strip = swap(other, 0, 1)
    along = lax.ppermute(mine, AXES, route(along_move))
    across = lax.ppermute(other, AXES, route(across_move))

    lon_masks, lat_masks = lons // 2, lats // 2
    blocks = {(0, 0): first}
    bit = lon_masks // 2
    while bit:
        for low, mask in list(blocks):
            blocks[low, mask ^ bit] = swap(blocks[low, mask], 0, 2 * bit)
        bit //= 2
    bit = 1
    while bit < lat_masks:
        for low, mask in list(blocks):
            blocks[low ^ bit, mask] = swap(blocks[low, mask], 2 * bit, 0)
        bit *= 2

    early = [block for (low, _), block in list(blocks.items())[:-1] if low == 1]
    deep = -(-(span + 1) * 3 * columns // LANES) * LANES
    band = call(
        functools.partial(band_kernel, reach),
        shape((rows // 2, 2 * bases * columns, deep)),
        [pltpu.VMEM((bases, rows, deep), jnp.float32)],
        1_000_000_000,
        held_filters,
        widths,
        after=(mine, *early[:1]),
    )
    features = call(
        functools.partial(feature_kernel, span),
        shape((bases, 2, rows, columns, half)),
        [pltpu.VMEM((rows + 2 * radius, 4, columns, half), jnp.bfloat16)],
        4_000_000_000,
        band,
        mine,
        pair_strip,
        along,
        across,
        after=early[1:],
    )
    features = features.reshape(bases, 2, rows * columns, half)

    points, width = rows * columns, out_columns // lat_masks
    keeps, gots = [], []
    for low in range(lat_masks):
        masks = [mask for held, mask in blocks if held == low]
        groups = [masks] if low == 0 else [masks[:-1], masks[-1:]]
        sources, pieces = [], []
        for held in groups:
            if not held:
                continue
            piece = call(
                stack_kernel,
                shape((len(held),) + block.shape),
                [],
                100_000,
                *[blocks[low, mask] for mask in held],
                after=(keeps[-1] if keeps and held == groups[-1] else features,),
            )
            sources += [(0, held), (1, held)]
            pieces += [piece, swap(piece, 1, 0)]
        keep, send = call(
            functools.partial(mix_kernel, sources),
            (shape((points, width), jnp.float32), shape((points, width))),
            [pltpu.VMEM((bases, 2 * lon_masks) + block.shape[1:], jnp.bfloat16)],
            2_000_000_000,
            features,
            *pieces,
        )
        keeps.append(keep)
        gots.append(swap(send, 0, 1))
    if width % LANES == 0:
        parts = [part for pair in zip(keeps, gots) for part in pair]
        out = call(
            functools.partial(finish_kernel, lat_masks),
            shape((points, out_columns)),
            [],
            10_000_000,
            *parts,
            mix_bias[None],
        )
        return out.reshape(rows, columns, out_columns)
    mixed = jnp.stack([keep + got.astype(jnp.float32) for keep, got in zip(keeps, gots)], 1)
    mixed = jnp.take(mixed, jnp.arange(lat_masks) ^ (lax.axis_index("lat") // 2), axis=1)
    mixed = mixed.reshape(rows, columns, out_columns) + mix_bias
    return jax.nn.gelu(mixed, approximate=False).astype(jnp.bfloat16)


def solution(mesh):
    placed = (
        P("lat", "lon", None),
        P(None, "lat", None, None),
        P("lat", None),
        P(None, None, ("lat", "lon")),
        P(),
    )
    return jax.shard_map(
        body, mesh=mesh, in_specs=placed, out_specs=P("lat", "lon", None), check_vma=False
    )
```

```python
import functools

import jax
import jax.numpy as jnp
from jax import lax
from jax.experimental import pallas as pl
from jax.experimental.pallas import tpu as pltpu
from jax.sharding import PartitionSpec as P


AXES = ("lat", "lon")
LANES = 128
HALF = LANES // 2
VMEM_BYTES = 20 * 1024 * 1024


def call(kernel, outs, scratch, *args, after=()):
    held = pl.BlockSpec(memory_space=pltpu.VMEM)
    count = len(args)

    def ordered(*refs):
        kernel(*refs[:count], *refs[count + len(after) :])

    return pl.pallas_call(
        ordered,
        out_shape=outs,
        in_specs=[held] * count + [pl.BlockSpec(memory_space=pl.ANY)] * len(after),
        out_specs=jax.tree.map(lambda _: held, outs),
        scratch_shapes=scratch,
        compiler_params=pltpu.CompilerParams(vmem_limit_bytes=VMEM_BYTES),
    )(*args, *after)


def shape(dims, dtype=jnp.bfloat16):
    return jax.ShapeDtypeStruct(dims, dtype)


def route(move):
    lats, lons = lax.axis_size("lat"), lax.axis_size("lon")
    pairs = []
    for lat in range(lats):
        for lon in range(lons):
            to_lat, to_lon = move(lat, lon, lats, lons)
            pairs.append((lat * lons + lon, to_lat * lons + to_lon))
    return pairs


def swap(block, lat_bits, lon_bits):
    return lax.ppermute(
        block, AXES, route(lambda lat, lon, lats, lons: (lat ^ lat_bits, lon ^ lon_bits))
    )


def outer_move(lat, lon, lats, lons):
    if lat == 0 or lat == lats - 1:
        return lat, (lon + lons // 2) % lons
    return (lat - 1 if lat % 2 == 0 else lat + 1), lon


def along_move(lat, lon, lats, lons):
    return lat, (lon + 2 if lon % 2 else lon - 2) % lons


def across_move(lat, lon, lats, lons):
    return lat, (lon + 1 if lon % 2 else lon - 1) % lons


def lane_of(value):
    return lax.broadcasted_iota(jnp.int32, value.shape, 1)


def turned(value, lanes):
    return pltpu.roll(value, lanes, 1)


def put(refs, odd, at, low, high):
    wide = low.shape[1]
    low, high = low.astype(jnp.bfloat16), high.astype(jnp.bfloat16)
    refs[0][:, at : at + wide] = jnp.where(odd == 1, high, low)
    refs[1][:, at : at + wide] = jnp.where(odd == 1, low, high)


def put_main(refs, odd, at, value, main):
    put(refs, odd, at, value[:, :main], value[:, main : 2 * main])


def split_of(value, main):
    return value[:, 2 * main : 2 * main + LANES].astype(jnp.float32)


def put_pair(refs, odd, at, first, second, main):
    put_main(refs, odd, at, first, main)
    put_main(refs, odd, at + main, second, main)
    first, second = split_of(first, main), split_of(second, main)
    front = lane_of(first) < HALF
    low = jnp.where(front, first, turned(second, HALF))
    high = jnp.where(front, turned(first, HALF), second)
    put(refs, odd, at + 2 * main, low, high)


def spare_of(tile, values, main, start):
    lane = lane_of(tile)
    for at, value in enumerate(values):
        last = value[:, 2 * main + LANES :].astype(jnp.float32)
        tile = jnp.where(lane == start + at, jnp.broadcast_to(last, tile.shape), tile)
    return tile


def start_kernel(main, w_ref, x_ref, own_ref, pair_ref, outer_ref, inner_ref):
    odd = lax.axis_index("lon") % 2
    refs = own_ref, pair_ref
    bases = w_ref.shape[0]
    values = [w_ref[k] for k in range(bases)]
    for k in range(0, bases - 1, 2):
        put_pair(refs, odd, k // 2 * (2 * main + LANES), values[k], values[k + 1], main)
    at = bases // 2 * (2 * main + LANES)
    put_main(refs, odd, at, values[-1], main)
    tile = split_of(values[-1], main)
    front = lane_of(tile) < HALF
    low, high = jnp.where(front, tile, 0.0), jnp.where(front, turned(tile, HALF), 0.0)
    put(refs, odd, at + main, low, spare_of(high, values, main, HALF))
    radius = outer_ref.shape[0]
    lower = lax.axis_index("lat") % 2
    low, high = x_ref[:radius], x_ref[-radius:]
    outer_ref[...] = jnp.where(lower == 1, high, low)
    inner_ref[...] = jnp.where(lower == 1, low, high)


def strip_kernel(main, x_ref, outer_ref, inner_ref, mine_ref, other_ref, rows_ref):
    lat, odd = lax.axis_index("lat"), lax.axis_index("lon") % 2
    pole = (lat == 0) | (lat == lax.axis_size("lat") - 1)
    radius, rows = outer_ref.shape[0], x_ref.shape[0]
    rows_ref[radius : radius + rows] = x_ref[...]
    far = radius + rows
    for r in range(radius):
        rows_ref[lat % 2 * far + r] = outer_ref[jnp.where(pole, radius - 1 - r, r)]
        rows_ref[(1 - lat % 2) * far + r] = inner_ref[r]
    refs = mine_ref, other_ref
    count = rows_ref.shape[0]
    values = [rows_ref[r] for r in range(count)]
    for r in range(count // 2):
        at = r * (2 * main + LANES)
        put_pair(refs, odd, at, values[r], values[r + count // 2], main)
    none = jnp.zeros((x_ref.shape[1], LANES), jnp.float32)
    put(refs, odd, count // 2 * (2 * main + LANES), none, spare_of(none, values, main, 0))


def join_kernel(mine_ref, other_ref, out_ref):
    odd = lax.axis_index("lon") % 2
    share = mine_ref.shape[0]
    low, high = mine_ref[...], other_ref[...]
    out_ref[:share] = jnp.where(odd == 1, high, low)
    out_ref[share:] = jnp.where(odd == 1, low, high)


def copy_kernel(source_ref, out_ref):
    out_ref[...] = source_ref[...]


def stack_kernel(*refs):
    for at, ref in enumerate(refs[:-1]):
        refs[-1][at] = ref[...]


def band_kernel(reach, f_ref, w_ref, band_ref, row_ref):
    bases, span, rows, taps = f_ref.shape
    columns = band_ref.shape[1] // (2 * bases)
    pitch = columns + taps - 1
    wide = band_ref.shape[2]
    offset = jnp.abs(lax.broadcasted_iota(jnp.int32, (rows, taps), 1) - reach)
    row_ref[...] = jnp.zeros_like(row_ref)
    for d in range(span):
        inside = offset <= w_ref[:, d : d + 1]
        for k in range(bases):
            tap = jnp.where(inside, f_ref[k, d].astype(jnp.float32), 0.0)
            row_ref[k, :, d * pitch : d * pitch + taps] = tap

    def one_pair(pair, _):
        for e in range(2):
            for k in range(bases):
                same = jnp.broadcast_to(row_ref[k, pl.ds(2 * pair + e, 1), :], (columns, wide))
                band = pltpu.roll(same, e * pitch, 1, stride=1, stride_axis=0)
                at = (e * bases + k) * columns
                band_ref[pair, at : at + columns, :] = band.astype(jnp.bfloat16)
        return 0

    lax.fori_loop(0, rows // 2, one_pair, 0)


def unpack(source_ref, slab_ref, slot, main):
    count = slab_ref.shape[0]
    wide = 2 * main + LANES
    spare = source_ref[:, count // 2 * wide :].astype(jnp.float32)
    lane = lane_of(spare)
    for r in range(count // 2):
        tile = source_ref[:, r * wide + 2 * main : (r + 1) * wide].astype(jnp.float32)
        for row, third in ((r, tile), (r + count // 2, turned(tile, HALF))):
            at = r * wide + (main if row > r else 0)
            slab_ref[row, slot, :, :main] = source_ref[:, at : at + main]
            last = turned(spare, (HALF - row) % LANES)
            third = jnp.where(lane == HALF, last, third)
            slab_ref[row, slot, :, main:] = third.astype(jnp.bfloat16)


def feature_kernel(span, band_ref, mine_ref, pair_ref, along_ref, across_ref, out_ref, slab_ref):
    odd = lax.axis_index("lon") % 2
    strips, rows, columns, _ = out_ref.shape
    half = slab_ref.shape[3]
    main = half - LANES
    unpack(mine_ref, slab_ref, 1 + odd, main)
    unpack(pair_ref, slab_ref, 2 - odd, main)
    unpack(along_ref, slab_ref, 3 * (1 - odd), main)
    unpack(across_ref, slab_ref, 3 * odd, main)
    bases = band_ref.shape[1] // (2 * columns)
    depth = (span + 1) * 3 * columns
    wide = 2 * main + LANES

    def one_pair(pair, _):
        band = band_ref[pair][:, :depth]
        source = [
            slab_ref[pl.ds(2 * pair, span + 1), strip : strip + 3].reshape(depth, half)
            for strip in range(strips)
        ]
        summed = jnp.dot(
            band, jnp.concatenate(source, axis=1), preferred_element_type=jnp.float32
        )
        for e in range(2):
            for strip in range(strips):

                def save(at, value):
                    out_ref[strip, 2 * pair + e, :, at : at + value.shape[1]] = value.astype(
                        jnp.bfloat16
                    )

                parts = []
                for k in range(bases):
                    at = (e * bases + k) * columns
                    parts.append(summed[at : at + columns, strip * half : (strip + 1) * half])
                lane = lane_of(parts[0][:, main:])
                for k, part in enumerate(parts):
                    save(k // 2 * wide + k % 2 * main, part[:, :main])
                for k in range(0, bases - 1, 2):
                    second = turned(parts[k + 1][:, main:], HALF)
                    save(k // 2 * wide + 2 * main, jnp.where(lane < HALF, parts[k][:, main:], second))
                tile = parts[-1][:, main:]
                for k in range(bases):
                    tile = jnp.where(lane == HALF + k, turned(parts[k][:, main:], k), tile)
                save(bases // 2 * wide + main, tile)
        return 0

    lax.fori_loop(0, rows // 2, one_pair, 0)


def strip_sum(feature_ref, strip, weight):
    return lax.dot_general(
        feature_ref[strip], weight, (((1,), (1,)), ((), ())), preferred_element_type=jnp.float32
    )


def mix_kernel(sources, feature_ref, *refs):
    piece_refs = refs[: len(sources)]
    keep_ref, send_ref, weight_ref = refs[len(sources) :]
    lat, lon = lax.axis_index("lat"), lax.axis_index("lon")
    odd = lon % 2
    masks = weight_ref.shape[0] // 2
    if sum(len(held) for _, held in sources) < 2 * masks:
        weight_ref[...] = jnp.zeros_like(weight_ref)
    for (core, held), ref in zip(sources, piece_refs):
        for at, mask in enumerate(held):
            place = (lat % 2 ^ core) * masks + ((lon // 2) ^ mask)
            weight_ref[place] = ref[at]
    weight = weight_ref[...].reshape(keep_ref.shape[1], weight_ref.shape[2])
    send_ref[...] = strip_sum(feature_ref, 1 - odd, weight).astype(send_ref.dtype)
    keep_ref[...] = strip_sum(feature_ref, odd, weight)


def rest_kernel(feature_ref, own_ref, crossed_ref, keep_ref, send_ref):
    odd = lax.axis_index("lon") % 2
    weight = jnp.concatenate([own_ref[0], crossed_ref[0]], axis=0)
    count = keep_ref.shape[0]
    for strip, ref in ((1 - odd, send_ref), (odd, keep_ref)):
        total = strip_sum(feature_ref, strip, weight)
        ref[...] = jnp.concatenate([total[:count], total[count:]], axis=1).astype(ref.dtype)


def finish_kernel(last, block, keep_ref, got_ref, keep2_ref, got2_ref, keep3_ref, got3_ref, bias_ref, out_ref):
    lat, lon = lax.axis_index("lat"), lax.axis_index("lon")
    wide = keep_ref.shape[1]

    def save(rows, at, total):
        at = pl.ds(pl.multiple_of(at, LANES), total.shape[1])
        total += bias_ref[:, at]
        grown = 0.5 * total * (1.0 + lax.erf(total * 0.5**0.5))
        out_ref[rows, at] = grown.astype(out_ref.dtype)

    save(slice(None), lat // 2 * wide, keep_ref[...] + got_ref[...].astype(jnp.float32))
    rest = keep3_ref[...] + got3_ref[...].astype(jnp.float32)
    count = rest.shape[0]
    lane = lane_of(rest)
    start = ((lon // 2) ^ last) * block
    inside = (lane >= start) & (lane < start + block)
    for crossed in range(2):
        core = lat % 2 ^ crossed
        at = pl.ds(pl.multiple_of(core * LANES, LANES), LANES)
        for part in range(2):
            rows = slice(part * count, (part + 1) * count)
            held = part * (2 * block) + crossed * block
            moved = pltpu.roll(rest, lax.rem(start - held + LANES, LANES), 1)
            total = keep2_ref[rows, at] + got2_ref[rows, at].astype(jnp.float32)
            total = jnp.where(inside, moved, total)
            save(rows, (1 - lat // 2) * wide + core * LANES, total)


def body(latent, filters, widths, mix_weight, mix_bias):
    lats, lons = lax.axis_size("lat"), lax.axis_size("lon")
    rows, columns, channels = latent.shape
    bases, _, span, taps = filters.shape
    radius, reach = span // 2, taps // 2
    assert reach == columns and rows % 2 == lats % 2 == lons % 2 == 0
    main = channels // (2 * LANES) * LANES
    assert channels == 2 * main + LANES + 1 and bases % 2 == 1
    assert bases <= HALF and rows + 2 * radius <= LANES
    half, packed = main + LANES, 2 * main + LANES
    out_columns, share = mix_bias.shape[0], mix_weight.shape[2]
    depth = bases // 2 * packed + half

    edge, halves = shape((radius, columns, channels)), shape((share, depth))
    weights = jnp.transpose(mix_weight, (0, 2, 1))
    own_weight, pair_weight, outer, inner = call(
        functools.partial(start_kernel, main), (halves, halves, edge, edge), [], weights, latent
    )
    got_weight = swap(pair_weight, 0, 1)
    from_outer = lax.ppermute(outer, AXES, route(outer_move))
    from_inner = swap(inner, 1, 0)
    block = shape((2 * share, depth))
    first = call(
        join_kernel, block, [], own_weight, got_weight, after=(from_outer, from_inner)
    )

    lon_masks, lat_masks = lons // 2, lats // 2
    steps = [1 << at for at in range(lat_masks.bit_length() - 1)]
    blocks = {(0, 0): first}
    bit = lon_masks // 2
    while bit:
        for low, mask in list(blocks):
            blocks[low, mask ^ bit] = swap(blocks[low, mask], 0, 2 * bit)
        bit //= 2
    order = [mask for _, mask in blocks]
    last = order[-1]
    for bit in steps:
        for low in range(bit):
            for mask in order[:-1]:
                blocks[low ^ bit, mask] = swap(blocks[low, mask], 2 * bit, 0)

    count = rows + 2 * radius
    strip = shape((columns, count // 2 * packed + LANES))
    mine, other = call(
        functools.partial(strip_kernel, main),
        (strip, strip),
        [pltpu.VMEM((count, columns, channels), jnp.bfloat16)],
        latent,
        from_outer,
        from_inner,
        after=tuple(blocks[bit, 0] for bit in steps),
    )
    pair_strip = swap(other, 0, 1)
    along = lax.ppermute(mine, AXES, route(along_move))
    across = lax.ppermute(other, AXES, route(across_move))
    deep = -(-(span + 1) * 3 * columns // LANES) * LANES
    band = call(
        functools.partial(band_kernel, reach),
        shape((rows // 2, 2 * bases * columns, deep)),
        [pltpu.VMEM((bases, rows, deep), jnp.float32)],
        jnp.transpose(filters, (0, 2, 1, 3)),
        widths,
        after=(mine,),
    )

    met = [value for key, value in blocks.items() if key != (0, last)]
    blocks[0, last] = call(
        copy_kernel, block, [], blocks[0, last], after=(*met, band, pair_strip, along, across)
    )
    for bit in steps:
        for low in range(bit):
            blocks[low ^ bit, last] = swap(blocks[low, last], 2 * bit, 0)
    features = call(
        functools.partial(feature_kernel, span),
        shape((2, rows, columns, depth)),
        [pltpu.VMEM((count, 4, columns, half), jnp.bfloat16)],
        band,
        mine,
        pair_strip,
        along,
        across,
        after=(blocks[0, last],),
    )
    features = features.reshape(2, rows * columns, depth)

    points, width = rows * columns, out_columns // lat_masks

    def stacked(low, held, after):
        piece = call(
            stack_kernel,
            shape((len(held),) + block.shape),
            [],
            *[blocks[low, mask] for mask in held],
            after=after,
        )
        return [piece, swap(piece, 1, 0)]

    def mixed(groups, pieces):
        sources = [(core, held) for held in groups for core in range(2)]
        keep, send = call(
            functools.partial(mix_kernel, sources),
            (shape((points, width), jnp.float32), shape((points, width))),
            [pltpu.VMEM((2 * lon_masks,) + block.shape, jnp.bfloat16)],
            features,
            *pieces,
        )
        return keep, swap(send, 0, 1)

    gate = (blocks[0, last],)
    if lat_masks == 2 and 8 * share == LANES == lon_masks * 2 * share and points % 2 == 0:
        parts = [*mixed([order], stacked(0, order, gate))]
        parts += mixed([order[:-1]], stacked(1, order[:-1], gate))
        rest = shape((points // 2, LANES), jnp.float32), shape((points // 2, LANES))
        keep, send = call(
            rest_kernel, rest, [], features, *stacked(1, order[-1:], (parts[2],))
        )
        out = call(
            functools.partial(finish_kernel, last, 2 * share),
            shape((points, out_columns)),
            [],
            *parts,
            keep,
            swap(send, 0, 1),
            mix_bias[None],
        )
        return out.reshape(rows, columns, out_columns)
    sums = []
    for low in range(lat_masks):
        keep, got = mixed([order], stacked(low, order, gate))
        sums.append(keep + got.astype(jnp.float32))
    total = jnp.stack(sums, 1)
    total = jnp.take(total, jnp.arange(lat_masks) ^ (lax.axis_index("lat") // 2), axis=1)
    total = total.reshape(rows, columns, out_columns) + mix_bias
    return jax.nn.gelu(total, approximate=False).astype(jnp.bfloat16)


def solution(mesh):
    placed = (
        P("lat", "lon", None),
        P(None, "lat", None, None),
        P("lat", None),
        P(None, None, ("lat", "lon")),
        P(),
    )
    return jax.shard_map(
        body, mesh=mesh, in_specs=placed, out_specs=P("lat", "lon", None), check_vma=False
    )
```

```python
import functools

import jax
import jax.numpy as jnp
from jax import lax
from jax.experimental import pallas as pl
from jax.experimental.pallas import tpu as pltpu
from jax.sharding import PartitionSpec as P


AXES = ("lat", "lon")
LANES = 128
HALF = LANES // 2
VMEM_BYTES = 20 * 1024 * 1024


def call(kernel, outs, scratch, *args, after=()):
    held = pl.BlockSpec(memory_space=pltpu.VMEM)
    count = len(args)

    def ordered(*refs):
        kernel(*refs[:count], *refs[count + len(after) :])

    return pl.pallas_call(
        ordered,
        out_shape=outs,
        in_specs=[held] * count + [pl.BlockSpec(memory_space=pl.ANY)] * len(after),
        out_specs=jax.tree.map(lambda _: held, outs),
        scratch_shapes=scratch,
        compiler_params=pltpu.CompilerParams(vmem_limit_bytes=VMEM_BYTES),
    )(*args, *after)


def shape(dims, dtype=jnp.bfloat16):
    return jax.ShapeDtypeStruct(dims, dtype)


def route(move):
    lats, lons = lax.axis_size("lat"), lax.axis_size("lon")
    pairs = []
    for lat in range(lats):
        for lon in range(lons):
            to_lat, to_lon = move(lat, lon, lats, lons)
            pairs.append((lat * lons + lon, to_lat * lons + to_lon))
    return pairs


def swap(block, lat_bits, lon_bits):
    return lax.ppermute(
        block, AXES, route(lambda lat, lon, lats, lons: (lat ^ lat_bits, lon ^ lon_bits))
    )


def outer_move(lat, lon, lats, lons):
    if lat == 0 or lat == lats - 1:
        return lat, (lon + lons // 2) % lons
    return (lat - 1 if lat % 2 == 0 else lat + 1), lon


def along_move(lat, lon, lats, lons):
    return lat, (lon + 2 if lon % 2 else lon - 2) % lons


def across_move(lat, lon, lats, lons):
    return lat, (lon + 1 if lon % 2 else lon - 1) % lons


def lane_of(value):
    return lax.broadcasted_iota(jnp.int32, value.shape, 1)


def turned(value, lanes):
    return pltpu.roll(value, lanes, 1)


def put(refs, odd, at, low, high):
    wide = low.shape[1]
    low, high = low.astype(jnp.bfloat16), high.astype(jnp.bfloat16)
    refs[0][:, at : at + wide] = jnp.where(odd == 1, high, low)
    refs[1][:, at : at + wide] = jnp.where(odd == 1, low, high)


def put_main(refs, odd, at, value, main):
    put(refs, odd, at, value[:, :main], value[:, main : 2 * main])


def split_of(value, main):
    return value[:, 2 * main : 2 * main + LANES].astype(jnp.float32)


def put_pair(refs, odd, at, first, second, main):
    put_main(refs, odd, at, first, main)
    put_main(refs, odd, at + main, second, main)
    first, second = split_of(first, main), split_of(second, main)
    front = lane_of(first) < HALF
    low = jnp.where(front, first, turned(second, HALF))
    high = jnp.where(front, turned(first, HALF), second)
    put(refs, odd, at + 2 * main, low, high)


def spare_of(tile, values, main, start):
    lane = lane_of(tile)
    for at, value in enumerate(values):
        last = value[:, 2 * main + LANES :].astype(jnp.float32)
        tile = jnp.where(lane == start + at, jnp.broadcast_to(last, tile.shape), tile)
    return tile


def weight_kernel(main, w_ref, own_ref, pair_ref):
    odd = lax.axis_index("lon") % 2
    refs = own_ref, pair_ref
    bases = w_ref.shape[0]
    values = [w_ref[k] for k in range(bases)]
    for k in range(0, bases - 1, 2):
        put_pair(refs, odd, k // 2 * (2 * main + LANES), values[k], values[k + 1], main)
    at = bases // 2 * (2 * main + LANES)
    put_main(refs, odd, at, values[-1], main)
    tile = split_of(values[-1], main)
    front = lane_of(tile) < HALF
    low, high = jnp.where(front, tile, 0.0), jnp.where(front, turned(tile, HALF), 0.0)
    put(refs, odd, at + main, low, spare_of(high, values, main, HALF))


def edge_kernel(x_ref, outer_ref, held_ref):
    radius = outer_ref.shape[0]
    lower = lax.axis_index("lat") % 2
    outer_ref[...] = jnp.where(lower == 1, x_ref[-radius:], x_ref[:radius])
    held_ref[...] = x_ref[...]


def start_kernel(main, w_ref, x_ref, own_ref, pair_ref, outer_ref, held_ref):
    weight_kernel(main, w_ref, own_ref, pair_ref)
    edge_kernel(x_ref, outer_ref, held_ref)


def strip_kernel(main, x_ref, outer_ref, mine_ref, other_ref, rows_ref):
    lat, odd = lax.axis_index("lat"), lax.axis_index("lon") % 2
    pole = (lat == 0) | (lat == lax.axis_size("lat") - 1)
    radius, rows = outer_ref.shape[0], x_ref.shape[0]
    rows_ref[pl.ds((1 - lat % 2) * radius, rows)] = x_ref[...]
    for r in range(radius):
        rows_ref[lat % 2 * rows + r] = outer_ref[jnp.where(pole, radius - 1 - r, r)]
    refs = mine_ref, other_ref
    count = rows_ref.shape[0]
    values = [rows_ref[r] for r in range(count)]
    for r in range(count // 2):
        at = r * (2 * main + LANES)
        put_pair(refs, odd, at, values[r], values[r + count // 2], main)
    none = jnp.zeros((x_ref.shape[1], LANES), jnp.float32)
    put(refs, odd, count // 2 * (2 * main + LANES), none, spare_of(none, values, main, 0))


def join_kernel(mine_ref, other_ref, out_ref):
    odd = lax.axis_index("lon") % 2
    share = mine_ref.shape[0]
    low, high = mine_ref[...], other_ref[...]
    out_ref[:share] = jnp.where(odd == 1, high, low)
    out_ref[share:] = jnp.where(odd == 1, low, high)


def copy_kernel(source_ref, out_ref):
    out_ref[...] = source_ref[...]


def stack_kernel(*refs):
    for at, ref in enumerate(refs[:-1]):
        refs[-1][at] = ref[...]


def band_kernel(reach, f_ref, w_ref, band_ref, row_ref):
    bases, span, rows, taps = f_ref.shape
    columns = band_ref.shape[1] // (2 * bases)
    pitch = columns + taps - 1
    wide = band_ref.shape[2]
    offset = jnp.abs(lax.broadcasted_iota(jnp.int32, (rows, taps), 1) - reach)
    row_ref[...] = jnp.zeros_like(row_ref)
    for d in range(span):
        inside = offset <= w_ref[:, d : d + 1]
        for k in range(bases):
            tap = jnp.where(inside, f_ref[k, d].astype(jnp.float32), 0.0)
            row_ref[k, :, d * pitch : d * pitch + taps] = tap

    def one_pair(pair, _):
        for e in range(2):
            for k in range(bases):
                same = jnp.broadcast_to(row_ref[k, pl.ds(2 * pair + e, 1), :], (columns, wide))
                band = pltpu.roll(same, e * pitch, 1, stride=1, stride_axis=0)
                at = (e * bases + k) * columns
                band_ref[pair, at : at + columns, :] = band.astype(jnp.bfloat16)
        return 0

    lax.fori_loop(0, rows // 2, one_pair, 0)


def unpack(source_ref, slab_ref, slot, main):
    count = slab_ref.shape[0]
    wide = 2 * main + LANES
    spare = source_ref[:, count // 2 * wide :].astype(jnp.float32)
    lane = lane_of(spare)
    for r in range(count // 2):
        tile = source_ref[:, r * wide + 2 * main : (r + 1) * wide].astype(jnp.float32)
        for row, third in ((r, tile), (r + count // 2, turned(tile, HALF))):
            at = r * wide + (main if row > r else 0)
            slab_ref[row, slot, :, :main] = source_ref[:, at : at + main]
            last = turned(spare, (HALF - row) % LANES)
            third = jnp.where(lane == HALF, last, third)
            slab_ref[row, slot, :, main:] = third.astype(jnp.bfloat16)


def slab_kernel(mine_ref, pair_ref, along_ref, across_ref, slab_ref, inner_ref):
    odd = lax.axis_index("lon") % 2
    main = slab_ref.shape[3] - LANES
    unpack(mine_ref, slab_ref, 1 + odd, main)
    unpack(pair_ref, slab_ref, 2 - odd, main)
    unpack(along_ref, slab_ref, 3 * (1 - odd), main)
    unpack(across_ref, slab_ref, 3 * odd, main)
    radius = inner_ref.shape[0]
    start = (1 - lax.axis_index("lat") % 2) * (slab_ref.shape[0] - radius)
    inner_ref[...] = slab_ref[pl.ds(start, radius)]


def feature_kernel(span, band_ref, rows_ref, inner_ref, out_ref, slab_ref):
    lower = lax.axis_index("lat") % 2
    held, radius = rows_ref.shape[0], inner_ref.shape[0]
    slab_ref[pl.ds(lower * radius, held)] = rows_ref[...]
    slab_ref[pl.ds((1 - lower) * held, radius)] = inner_ref[...]
    strips, rows, columns, _ = out_ref.shape
    half = slab_ref.shape[3]
    main = half - LANES
    bases = band_ref.shape[1] // (2 * columns)
    depth = (span + 1) * 3 * columns
    wide = 2 * main + LANES

    def one_pair(pair, _):
        band = band_ref[pair][:, :depth]
        source = [
            slab_ref[pl.ds(2 * pair, span + 1), strip : strip + 3].reshape(depth, half)
            for strip in range(strips)
        ]
        summed = jnp.dot(
            band, jnp.concatenate(source, axis=1), preferred_element_type=jnp.float32
        )
        for e in range(2):
            for strip in range(strips):

                def save(at, value):
                    out_ref[strip, 2 * pair + e, :, at : at + value.shape[1]] = value.astype(
                        jnp.bfloat16
                    )

                parts = []
                for k in range(bases):
                    at = (e * bases + k) * columns
                    parts.append(summed[at : at + columns, strip * half : (strip + 1) * half])
                lane = lane_of(parts[0][:, main:])
                for k, part in enumerate(parts):
                    save(k // 2 * wide + k % 2 * main, part[:, :main])
                for k in range(0, bases - 1, 2):
                    second = turned(parts[k + 1][:, main:], HALF)
                    save(k // 2 * wide + 2 * main, jnp.where(lane < HALF, parts[k][:, main:], second))
                tile = parts[-1][:, main:]
                for k in range(bases):
                    tile = jnp.where(lane == HALF + k, turned(parts[k][:, main:], k), tile)
                save(bases // 2 * wide + main, tile)
        return 0

    lax.fori_loop(0, rows // 2, one_pair, 0)


def product(feature_ref, strip, weight):
    return lax.dot_general(
        feature_ref[strip], weight, (((1,), (1,)), ((), ())), preferred_element_type=jnp.float32
    )


def partner_mix_kernel(sources, feature_ref, *refs):
    piece_refs = refs[: len(sources)]
    send_ref, weight_ref = refs[len(sources) :]
    lat, lon = lax.axis_index("lat"), lax.axis_index("lon")
    masks = lax.axis_size("lon") // 2
    if sum(len(held) for _, _, held in sources) < weight_ref.shape[0]:
        weight_ref[...] = jnp.zeros_like(weight_ref)
    for (core, low, held), ref in zip(sources, piece_refs):
        row = 2 * ((lat // 2) ^ low) + (lat % 2 ^ core)
        for at, mask in enumerate(held):
            weight_ref[row * masks + ((lon // 2) ^ mask)] = ref[at]
    weight = weight_ref[...].reshape(send_ref.shape[1], weight_ref.shape[2])
    send_ref[...] = product(feature_ref, 1 - lon % 2, weight).astype(send_ref.dtype)


def own_mix_kernel(feature_ref, weight_ref, keep_ref):
    weight = weight_ref[...].reshape(keep_ref.shape[1], weight_ref.shape[2])
    keep_ref[...] = product(feature_ref, lax.axis_index("lon") % 2, weight)


def rest_kernel(feature_ref, own_ref, crossed_ref, keep_ref, send_ref):
    odd = lax.axis_index("lon") % 2
    weight = jnp.concatenate([own_ref[0], crossed_ref[0]], axis=0)
    count = keep_ref.shape[0]
    for strip, ref in ((1 - odd, send_ref), (odd, keep_ref)):
        total = product(feature_ref, strip, weight)
        ref[...] = jnp.concatenate([total[:count], total[count:]], axis=1).astype(ref.dtype)


def finish_kernel(last, block, keep_ref, got_ref, keep2_ref, got2_ref, bias_ref, out_ref):
    lat, lon = lax.axis_index("lat"), lax.axis_index("lon")
    wide = out_ref.shape[1] // 2

    def save(rows, at, total):
        total += bias_ref[:, at]
        grown = 0.5 * total * (1.0 + lax.erf(total * 0.5**0.5))
        out_ref[rows, at] = grown.astype(out_ref.dtype)

    at = pl.ds(pl.multiple_of(lat // 2 * wide, LANES), wide)
    save(slice(None), at, keep_ref[:, at] + got_ref[:, at].astype(jnp.float32))
    rest = keep2_ref[...] + got2_ref[...].astype(jnp.float32)
    count = rest.shape[0]
    lane = lane_of(rest)
    start = ((lon // 2) ^ last) * block
    inside = (lane >= start) & (lane < start + block)
    for crossed in range(2):
        tile = (1 - lat // 2) * 2 + (lat % 2 ^ crossed)
        at = pl.ds(pl.multiple_of(tile * LANES, LANES), LANES)
        for part in range(2):
            rows = slice(part * count, (part + 1) * count)
            held = part * (2 * block) + crossed * block
            moved = pltpu.roll(rest, lax.rem(start - held + LANES, LANES), 1)
            total = keep_ref[rows, at] + got_ref[rows, at].astype(jnp.float32)
            save(rows, at, jnp.where(inside, moved, total))


def body(latent, filters, widths, mix_weight, mix_bias):
    lats, lons = lax.axis_size("lat"), lax.axis_size("lon")
    rows, columns, channels = latent.shape
    bases, _, span, taps = filters.shape
    radius, reach = span // 2, taps // 2
    assert reach == columns and rows % 2 == lats % 2 == lons % 2 == 0
    main = channels // (2 * LANES) * LANES
    assert channels == 2 * main + LANES + 1 and bases % 2 == 1
    assert bases <= HALF and rows + 2 * radius <= LANES
    half, packed = main + LANES, 2 * main + LANES
    out_columns, share = mix_bias.shape[0], mix_weight.shape[2]
    depth = bases // 2 * packed + half

    edge, halves = shape((radius, columns, channels)), shape((share, depth))
    weights = jnp.transpose(mix_weight, (0, 2, 1))
    own_weight, pair_weight = call(
        functools.partial(weight_kernel, main), (halves, halves), [], weights
    )
    outer, held_latent = call(edge_kernel, (edge, shape(latent.shape)), [], latent)
    got_weight = swap(pair_weight, 0, 1)
    from_outer = lax.ppermute(outer, AXES, route(outer_move))
    block = shape((2 * share, depth))
    first = call(join_kernel, block, [], own_weight, got_weight)

    lon_masks, lat_masks = lons // 2, lats // 2
    steps = [1 << at for at in range(lat_masks.bit_length() - 1)]
    blocks = {(0, 0): first}
    bit = lon_masks // 2
    while bit:
        for low, mask in list(blocks):
            blocks[low, mask ^ bit] = swap(blocks[low, mask], 0, 2 * bit)
        bit //= 2
    order = [mask for _, mask in blocks]
    last = order[-1]
    count = rows + radius
    strip = shape((columns, count // 2 * packed + LANES))

    def cross(masks):
        for bit in steps:
            for low in range(bit):
                for mask in masks:
                    blocks[low ^ bit, mask] = swap(blocks[low, mask], 2 * bit, 0)

    cross(order[:1])
    crossed_first = tuple(blocks[bit, 0] for bit in steps)
    mine, other = call(
        functools.partial(strip_kernel, main),
        (strip, strip),
        [pltpu.VMEM((count, columns, channels), jnp.bfloat16)],
        held_latent,
        from_outer,
    )
    for mask in order[1:-1]:
        blocks[0, mask] = call(copy_kernel, block, [], blocks[0, mask], after=(mine,))
    cross(order[1:-1])
    pair_strip = swap(other, 0, 1)
    along = lax.ppermute(mine, AXES, route(along_move))
    across = lax.ppermute(other, AXES, route(across_move))
    deep = -(-(span + 1) * 3 * columns // LANES) * LANES
    band = call(
        functools.partial(band_kernel, reach),
        shape((rows // 2, 2 * bases * columns, deep)),
        [pltpu.VMEM((bases, rows, deep), jnp.float32)],
        jnp.transpose(filters, (0, 2, 1, 3)),
        widths,
        after=(pair_strip,),
    )
    slab, inner = call(
        slab_kernel,
        (shape((count, 4, columns, half)), shape((radius, 4, columns, half))),
        [],
        mine,
        pair_strip,
        along,
        across,
    )
    from_inner = swap(inner, 1, 0)

    features = call(
        functools.partial(feature_kernel, span),
        shape((2, rows, columns, depth)),
        [pltpu.VMEM((rows + 2 * radius, 4, columns, half), jnp.bfloat16)],
        band,
        slab,
        from_inner,
    )
    features = features.reshape(2, rows * columns, depth)
    met = [value for key, value in blocks.items() if key != (0, last)]
    blocks[0, last] = call(
        copy_kernel, block, [], blocks[0, last], after=(*met, band, *(features,))
    )
    cross(order[-1:])
    points = rows * columns

    def stacked(low, held, after):
        piece = call(
            stack_kernel,
            shape((len(held),) + block.shape),
            [],
            *[blocks[low, mask] for mask in held],
            after=after,
        )
        return [piece, swap(piece, 1, 0)]

    apart = lat_masks == 2 and 8 * share == LANES == lon_masks * 2 * share and points % 2 == 0
    sources, pieces = [], []
    for low in range(lat_masks):
        held = order[:-1] if low and apart else order
        sources += [(core, low, held) for core in range(2)]
        pieces += stacked(low, held, (blocks[0, last],) if low == 0 else (blocks[0, last],))
    send, weight = call(
        functools.partial(partner_mix_kernel, sources),
        (shape((points, out_columns)), shape((lats * lon_masks,) + block.shape)),
        [],
        features,
        *pieces,
    )
    got = swap(send, 0, 1)
    sums = shape((points, out_columns), jnp.float32)
    if not apart:
        keep = call(own_mix_kernel, sums, [], features, weight)
        total = (keep + got.astype(jnp.float32)).reshape(rows, columns, out_columns) + mix_bias
        return jax.nn.gelu(total, approximate=False).astype(jnp.bfloat16)
    rest = shape((points // 2, LANES), jnp.float32), shape((points // 2, LANES))
    rest_keep, rest_send = call(
        rest_kernel, rest, [], features, *stacked(1, order[-1:], (send,))
    )
    rest_got = swap(rest_send, 0, 1)
    keep = call(own_mix_kernel, sums, [], features, weight)
    out = call(
        functools.partial(finish_kernel, last, 2 * share),
        shape((points, out_columns)),
        [],
        keep,
        got,
        rest_keep,
        rest_got,
        mix_bias[None],
    )
    return out.reshape(rows, columns, out_columns)


def solution(mesh):
    placed = (
        P("lat", "lon", None),
        P(None, "lat", None, None),
        P("lat", None),
        P(None, None, ("lat", "lon")),
        P(),
    )
    return jax.shard_map(
        body, mesh=mesh, in_specs=placed, out_specs=P("lat", "lon", None), check_vma=False
    )
```

```python
import functools

import jax
import jax.numpy as jnp
from jax import lax
from jax.experimental import pallas as pl
from jax.experimental.pallas import tpu as pltpu
from jax.sharding import PartitionSpec as P


AXES = ("lat", "lon")
LANES = 128
HALF = LANES // 2
VMEM_BYTES = 20 * 1024 * 1024


def call(kernel, outs, scratch, *args, after=()):
    held = pl.BlockSpec(memory_space=pltpu.VMEM)
    count = len(args)

    def ordered(*refs):
        kernel(*refs[:count], *refs[count + len(after) :])

    return pl.pallas_call(
        ordered,
        out_shape=outs,
        in_specs=[held] * count + [pl.BlockSpec(memory_space=pl.ANY)] * len(after),
        out_specs=jax.tree.map(lambda _: held, outs),
        scratch_shapes=scratch,
        compiler_params=pltpu.CompilerParams(vmem_limit_bytes=VMEM_BYTES),
    )(*args, *after)


def shape(dims, dtype=jnp.bfloat16):
    return jax.ShapeDtypeStruct(dims, dtype)


def route(move):
    lats, lons = lax.axis_size("lat"), lax.axis_size("lon")
    pairs = []
    for lat in range(lats):
        for lon in range(lons):
            to_lat, to_lon = move(lat, lon, lats, lons)
            pairs.append((lat * lons + lon, to_lat * lons + to_lon))
    return pairs


def swap(block, lat_bits, lon_bits):
    return lax.ppermute(
        block, AXES, route(lambda lat, lon, lats, lons: (lat ^ lat_bits, lon ^ lon_bits))
    )


def outer_move(lat, lon, lats, lons):
    if lat == 0 or lat == lats - 1:
        return lat, (lon + lons // 2) % lons
    return (lat - 1 if lat % 2 == 0 else lat + 1), lon


def along_move(lat, lon, lats, lons):
    return lat, (lon + 2 if lon % 2 else lon - 2) % lons


def across_move(lat, lon, lats, lons):
    return lat, (lon + 1 if lon % 2 else lon - 1) % lons


def lane_of(value):
    return lax.broadcasted_iota(jnp.int32, value.shape, 1)


def turned(value, lanes):
    return pltpu.roll(value, lanes, 1)


def put(refs, odd, at, low, high):
    wide = low.shape[1]
    low, high = low.astype(jnp.bfloat16), high.astype(jnp.bfloat16)
    refs[0][:, at : at + wide] = jnp.where(odd == 1, high, low)
    refs[1][:, at : at + wide] = jnp.where(odd == 1, low, high)


def put_main(refs, odd, at, value, main):
    put(refs, odd, at, value[:, :main], value[:, main : 2 * main])


def split_of(value, main):
    return value[:, 2 * main : 2 * main + LANES].astype(jnp.float32)


def put_pair(refs, odd, at, first, second, main):
    put_main(refs, odd, at, first, main)
    put_main(refs, odd, at + main, second, main)
    first, second = split_of(first, main), split_of(second, main)
    front = lane_of(first) < HALF
    low = jnp.where(front, first, turned(second, HALF))
    high = jnp.where(front, turned(first, HALF), second)
    put(refs, odd, at + 2 * main, low, high)


def spare_of(tile, values, main, start):
    lane = lane_of(tile)
    for at, value in enumerate(values):
        last = value[:, 2 * main + LANES :].astype(jnp.float32)
        tile = jnp.where(lane == start + at, jnp.broadcast_to(last, tile.shape), tile)
    return tile


def weight_kernel(main, w_ref, own_ref, pair_ref):
    odd = lax.axis_index("lon") % 2
    refs = own_ref, pair_ref
    bases = w_ref.shape[0]
    values = [w_ref[k] for k in range(bases)]
    for k in range(0, bases - 1, 2):
        put_pair(refs, odd, k // 2 * (2 * main + LANES), values[k], values[k + 1], main)
    at = bases // 2 * (2 * main + LANES)
    put_main(refs, odd, at, values[-1], main)
    tile = split_of(values[-1], main)
    front = lane_of(tile) < HALF
    low, high = jnp.where(front, tile, 0.0), jnp.where(front, turned(tile, HALF), 0.0)
    put(refs, odd, at + main, low, spare_of(high, values, main, HALF))


def edge_kernel(x_ref, outer_ref, held_ref):
    radius = outer_ref.shape[0]
    lower = lax.axis_index("lat") % 2
    outer_ref[...] = jnp.where(lower == 1, x_ref[-radius:], x_ref[:radius])
    held_ref[...] = x_ref[...]


def start_kernel(main, w_ref, x_ref, own_ref, pair_ref, outer_ref, held_ref):
    weight_kernel(main, w_ref, own_ref, pair_ref)
    edge_kernel(x_ref, outer_ref, held_ref)


def strip_kernel(main, x_ref, outer_ref, mine_ref, other_ref, rows_ref):
    lat, odd = lax.axis_index("lat"), lax.axis_index("lon") % 2
    pole = (lat == 0) | (lat == lax.axis_size("lat") - 1)
    radius, rows = outer_ref.shape[0], x_ref.shape[0]
    rows_ref[pl.ds((1 - lat % 2) * radius, rows)] = x_ref[...]
    for r in range(radius):
        rows_ref[lat % 2 * rows + r] = outer_ref[jnp.where(pole, radius - 1 - r, r)]
    refs = mine_ref, other_ref
    count = rows_ref.shape[0]
    values = [rows_ref[r] for r in range(count)]
    for r in range(count // 2):
        at = r * (2 * main + LANES)
        put_pair(refs, odd, at, values[r], values[r + count // 2], main)
    none = jnp.zeros((x_ref.shape[1], LANES), jnp.float32)
    put(refs, odd, count // 2 * (2 * main + LANES), none, spare_of(none, values, main, 0))


def join_kernel(mine_ref, other_ref, out_ref):
    odd = lax.axis_index("lon") % 2
    share = mine_ref.shape[0]
    low, high = mine_ref[...], other_ref[...]
    out_ref[:share] = jnp.where(odd == 1, high, low)
    out_ref[share:] = jnp.where(odd == 1, low, high)


def copy_kernel(source_ref, out_ref):
    out_ref[...] = source_ref[...]


def stack_kernel(*refs):
    for at, ref in enumerate(refs[:-1]):
        refs[-1][at] = ref[...]


def band_kernel(reach, f_ref, w_ref, band_ref, row_ref):
    bases, span, rows, taps = f_ref.shape
    columns = band_ref.shape[1] // (2 * bases)
    pitch = columns + taps - 1
    wide = band_ref.shape[2]
    offset = jnp.abs(lax.broadcasted_iota(jnp.int32, (rows, taps), 1) - reach)
    row_ref[...] = jnp.zeros_like(row_ref)
    for d in range(span):
        inside = offset <= w_ref[:, d : d + 1]
        for k in range(bases):
            tap = jnp.where(inside, f_ref[k, d].astype(jnp.float32), 0.0)
            row_ref[k, :, d * pitch : d * pitch + taps] = tap

    def one_pair(pair, _):
        for e in range(2):
            for k in range(bases):
                same = jnp.broadcast_to(row_ref[k, pl.ds(2 * pair + e, 1), :], (columns, wide))
                band = pltpu.roll(same, e * pitch, 1, stride=1, stride_axis=0)
                at = (e * bases + k) * columns
                band_ref[pair, at : at + columns, :] = band.astype(jnp.bfloat16)
        return 0

    lax.fori_loop(0, rows // 2, one_pair, 0)


def unpack(source_ref, slab_ref, slot, main):
    count = slab_ref.shape[0]
    wide = 2 * main + LANES
    spare = source_ref[:, count // 2 * wide :].astype(jnp.float32)
    lane = lane_of(spare)
    for r in range(count // 2):
        tile = source_ref[:, r * wide + 2 * main : (r + 1) * wide].astype(jnp.float32)
        for row, third in ((r, tile), (r + count // 2, turned(tile, HALF))):
            at = r * wide + (main if row > r else 0)
            slab_ref[row, slot, :, :main] = source_ref[:, at : at + main]
            last = turned(spare, (HALF - row) % LANES)
            third = jnp.where(lane == HALF, last, third)
            slab_ref[row, slot, :, main:] = third.astype(jnp.bfloat16)


def slab_kernel(mine_ref, pair_ref, along_ref, across_ref, slab_ref, inner_ref):
    odd = lax.axis_index("lon") % 2
    main = slab_ref.shape[3] - LANES
    unpack(mine_ref, slab_ref, 1 + odd, main)
    unpack(pair_ref, slab_ref, 2 - odd, main)
    unpack(along_ref, slab_ref, 3 * (1 - odd), main)
    unpack(across_ref, slab_ref, 3 * odd, main)
    radius = inner_ref.shape[0]
    start = (1 - lax.axis_index("lat") % 2) * (slab_ref.shape[0] - radius)
    inner_ref[...] = slab_ref[pl.ds(start, radius)]


def feature_kernel(span, band_ref, rows_ref, inner_ref, out_ref, slab_ref):
    lower = lax.axis_index("lat") % 2
    held, radius = rows_ref.shape[0], inner_ref.shape[0]
    slab_ref[pl.ds(lower * radius, held)] = rows_ref[...]
    slab_ref[pl.ds((1 - lower) * held, radius)] = inner_ref[...]
    strips, rows, columns, _ = out_ref.shape
    half = slab_ref.shape[3]
    main = half - LANES
    bases = band_ref.shape[1] // (2 * columns)
    depth = (span + 1) * 3 * columns
    wide = 2 * main + LANES

    def one_pair(pair, _):
        band = band_ref[pair][:, :depth]
        source = [
            slab_ref[pl.ds(2 * pair, span + 1), strip : strip + 3].reshape(depth, half)
            for strip in range(strips)
        ]
        summed = jnp.dot(
            band, jnp.concatenate(source, axis=1), preferred_element_type=jnp.float32
        )
        for e in range(2):
            for strip in range(strips):

                def save(at, value):
                    out_ref[strip, 2 * pair + e, :, at : at + value.shape[1]] = value.astype(
                        jnp.bfloat16
                    )

                parts = []
                for k in range(bases):
                    at = (e * bases + k) * columns
                    parts.append(summed[at : at + columns, strip * half : (strip + 1) * half])
                lane = lane_of(parts[0][:, main:])
                for k, part in enumerate(parts):
                    save(k // 2 * wide + k % 2 * main, part[:, :main])
                for k in range(0, bases - 1, 2):
                    second = turned(parts[k + 1][:, main:], HALF)
                    save(k // 2 * wide + 2 * main, jnp.where(lane < HALF, parts[k][:, main:], second))
                tile = parts[-1][:, main:]
                for k in range(bases):
                    tile = jnp.where(lane == HALF + k, turned(parts[k][:, main:], k), tile)
                save(bases // 2 * wide + main, tile)
        return 0

    lax.fori_loop(0, rows // 2, one_pair, 0)


def product(feature_ref, strip, weight):
    return lax.dot_general(
        feature_ref[strip], weight, (((1,), (1,)), ((), ())), preferred_element_type=jnp.float32
    )


def partner_mix_kernel(sources, feature_ref, *refs):
    piece_refs = refs[: len(sources)]
    send_ref, weight_ref = refs[len(sources) :]
    lat, lon = lax.axis_index("lat"), lax.axis_index("lon")
    masks = lax.axis_size("lon") // 2
    if sum(len(held) for _, _, held in sources) < weight_ref.shape[0]:
        weight_ref[...] = jnp.zeros_like(weight_ref)
    for (core, low, held), ref in zip(sources, piece_refs):
        row = 2 * ((lat // 2) ^ low) + (lat % 2 ^ core)
        for at, mask in enumerate(held):
            weight_ref[row * masks + ((lon // 2) ^ mask)] = ref[at]
    weight = weight_ref[...].reshape(send_ref.shape[1], weight_ref.shape[2])
    send_ref[...] = product(feature_ref, 1 - lon % 2, weight).astype(send_ref.dtype)


def own_mix_kernel(feature_ref, weight_ref, keep_ref):
    weight = weight_ref[...].reshape(keep_ref.shape[1], weight_ref.shape[2])
    keep_ref[...] = product(feature_ref, lax.axis_index("lon") % 2, weight)


def rest_kernel(own, feature_ref, own_ref, crossed_ref, sum_ref):
    odd = lax.axis_index("lon") % 2
    weight = jnp.concatenate([own_ref[0], crossed_ref[0]], axis=0)
    count = sum_ref.shape[0]
    total = product(feature_ref, odd if own else 1 - odd, weight)
    sum_ref[...] = jnp.concatenate([total[:count], total[count:]], axis=1).astype(sum_ref.dtype)


def finish_kernel(last, block, keep_ref, got_ref, keep2_ref, got2_ref, bias_ref, out_ref):
    lat, lon = lax.axis_index("lat"), lax.axis_index("lon")
    wide = out_ref.shape[1] // 2

    def save(rows, at, total):
        total += bias_ref[:, at]
        grown = 0.5 * total * (1.0 + lax.erf(total * 0.5**0.5))
        out_ref[rows, at] = grown.astype(out_ref.dtype)

    at = pl.ds(pl.multiple_of(lat // 2 * wide, LANES), wide)
    save(slice(None), at, keep_ref[:, at] + got_ref[:, at].astype(jnp.float32))
    rest = keep2_ref[...] + got2_ref[...].astype(jnp.float32)
    count = rest.shape[0]
    lane = lane_of(rest)
    start = ((lon // 2) ^ last) * block
    inside = (lane >= start) & (lane < start + block)
    for crossed in range(2):
        tile = (1 - lat // 2) * 2 + (lat % 2 ^ crossed)
        at = pl.ds(pl.multiple_of(tile * LANES, LANES), LANES)
        for part in range(2):
            rows = slice(part * count, (part + 1) * count)
            held = part * (2 * block) + crossed * block
            moved = pltpu.roll(rest, lax.rem(start - held + LANES, LANES), 1)
            total = keep_ref[rows, at] + got_ref[rows, at].astype(jnp.float32)
            save(rows, at, jnp.where(inside, moved, total))


def body(latent, filters, widths, mix_weight, mix_bias):
    lats, lons = lax.axis_size("lat"), lax.axis_size("lon")
    rows, columns, channels = latent.shape
    bases, _, span, taps = filters.shape
    radius, reach = span // 2, taps // 2
    assert reach == columns and rows % 2 == lats % 2 == lons % 2 == 0
    main = channels // (2 * LANES) * LANES
    assert channels == 2 * main + LANES + 1 and bases % 2 == 1
    assert bases <= HALF and rows + 2 * radius <= LANES
    half, packed = main + LANES, 2 * main + LANES
    out_columns, share = mix_bias.shape[0], mix_weight.shape[2]
    depth = bases // 2 * packed + half

    edge, halves = shape((radius, columns, channels)), shape((share, depth))
    weights = jnp.transpose(mix_weight, (0, 2, 1))
    own_weight, pair_weight = call(
        functools.partial(weight_kernel, main), (halves, halves), [], weights
    )
    outer, held_latent = call(edge_kernel, (edge, shape(latent.shape)), [], latent)
    got_weight = swap(pair_weight, 0, 1)
    from_outer = lax.ppermute(outer, AXES, route(outer_move))
    block = shape((2 * share, depth))
    first = call(join_kernel, block, [], own_weight, got_weight)

    lon_masks, lat_masks = lons // 2, lats // 2
    steps = [1 << at for at in range(lat_masks.bit_length() - 1)]
    blocks = {(0, 0): first}
    bit = lon_masks // 2
    while bit:
        for low, mask in list(blocks):
            blocks[low, mask ^ bit] = swap(blocks[low, mask], 0, 2 * bit)
        bit //= 2
    order = [mask for _, mask in blocks]
    last = order[-1]
    count = rows + radius
    strip = shape((columns, count // 2 * packed + LANES))

    def cross(masks):
        for bit in steps:
            for low in range(bit):
                for mask in masks:
                    blocks[low ^ bit, mask] = swap(blocks[low, mask], 2 * bit, 0)

    cross(order[:1])
    mine, other = call(
        functools.partial(strip_kernel, main),
        (strip, strip),
        [pltpu.VMEM((count, columns, channels), jnp.bfloat16)],
        held_latent,
        from_outer,
    )
    for mask in order[1:-1]:
        blocks[0, mask] = call(copy_kernel, block, [], blocks[0, mask], after=(mine,))
    cross(order[1:-1])
    pair_strip = swap(other, 0, 1)
    along = lax.ppermute(mine, AXES, route(along_move))
    across = lax.ppermute(other, AXES, route(across_move))
    deep = -(-(span + 1) * 3 * columns // LANES) * LANES
    band = call(
        functools.partial(band_kernel, reach),
        shape((rows // 2, 2 * bases * columns, deep)),
        [pltpu.VMEM((bases, rows, deep), jnp.float32)],
        jnp.transpose(filters, (0, 2, 1, 3)),
        widths,
        after=(pair_strip,),
    )
    slab, inner = call(
        slab_kernel,
        (shape((count, 4, columns, half)), shape((radius, 4, columns, half))),
        [],
        mine,
        pair_strip,
        along,
        across,
    )
    from_inner = swap(inner, 1, 0)

    features = call(
        functools.partial(feature_kernel, span),
        shape((2, rows, columns, depth)),
        [pltpu.VMEM((rows + 2 * radius, 4, columns, half), jnp.bfloat16)],
        band,
        slab,
        from_inner,
    )
    features = features.reshape(2, rows * columns, depth)
    met = [value for key, value in blocks.items() if key != (0, last)]
    blocks[0, last] = call(
        copy_kernel, block, [], blocks[0, last], after=(*met, features)
    )
    cross(order[-1:])
    points = rows * columns

    def stacked(low, held, after):
        piece = call(
            stack_kernel,
            shape((len(held),) + block.shape),
            [],
            *[blocks[low, mask] for mask in held],
            after=after,
        )
        return [piece, swap(piece, 1, 0)]

    apart = lat_masks == 2 and 8 * share == LANES == lon_masks * 2 * share and points % 2 == 0
    sources, pieces = [], []
    for low in range(lat_masks):
        held = order[:-1] if low and apart else order
        sources += [(core, low, held) for core in range(2)]
        pieces += stacked(low, held, (blocks[0, last],) if low == 0 else (blocks[0, last],))
    send, weight = call(
        functools.partial(partner_mix_kernel, sources),
        (shape((points, out_columns)), shape((lats * lon_masks,) + block.shape)),
        [],
        features,
        *pieces,
    )
    got = swap(send, 0, 1)
    sums = shape((points, out_columns), jnp.float32)
    if not apart:
        keep = call(own_mix_kernel, sums, [], features, weight)
        total = (keep + got.astype(jnp.float32)).reshape(rows, columns, out_columns) + mix_bias
        return jax.nn.gelu(total, approximate=False).astype(jnp.bfloat16)
    rest, pieces = (points // 2, LANES), stacked(1, order[-1:], (send,))
    rest_send = call(
        functools.partial(rest_kernel, False), shape(rest), [], features, *pieces
    )
    rest_got = swap(rest_send, 0, 1)
    keep = call(own_mix_kernel, sums, [], features, weight, after=(rest_send,))
    rest_keep = call(
        functools.partial(rest_kernel, True),
        shape(rest, jnp.float32),
        [],
        features,
        *pieces,
        after=(rest_send,),
    )
    out = call(
        functools.partial(finish_kernel, last, 2 * share),
        shape((points, out_columns)),
        [],
        keep,
        got,
        rest_keep,
        rest_got,
        mix_bias[None],
    )
    return out.reshape(rows, columns, out_columns)


def solution(mesh):
    placed = (
        P("lat", "lon", None),
        P(None, "lat", None, None),
        P("lat", None),
        P(None, None, ("lat", "lon")),
        P(),
    )
    return jax.shard_map(
        body, mesh=mesh, in_specs=placed, out_specs=P("lat", "lon", None), check_vma=False
    )
```

```python
import functools

import jax
import jax.numpy as jnp
from jax import lax
from jax.experimental import pallas as pl
from jax.experimental.pallas import tpu as pltpu
from jax.sharding import PartitionSpec as P


AXES = ("lat", "lon")
LANES = 128
HALF = LANES // 2
VMEM_BYTES = 20 * 1024 * 1024


def call(kernel, outs, scratch, *args, after=()):
    held = pl.BlockSpec(memory_space=pltpu.VMEM)
    count = len(args)

    def ordered(*refs):
        kernel(*refs[:count], *refs[count + len(after) :])

    return pl.pallas_call(
        ordered,
        out_shape=outs,
        in_specs=[held] * count + [pl.BlockSpec(memory_space=pl.ANY)] * len(after),
        out_specs=jax.tree.map(lambda _: held, outs),
        scratch_shapes=scratch,
        compiler_params=pltpu.CompilerParams(vmem_limit_bytes=VMEM_BYTES),
    )(*args, *after)


def shape(dims, dtype=jnp.bfloat16):
    return jax.ShapeDtypeStruct(dims, dtype)


def route(move):
    lats, lons = lax.axis_size("lat"), lax.axis_size("lon")
    pairs = []
    for lat in range(lats):
        for lon in range(lons):
            to_lat, to_lon = move(lat, lon, lats, lons)
            pairs.append((lat * lons + lon, to_lat * lons + to_lon))
    return pairs


def swap(block, lat_bits, lon_bits):
    return lax.ppermute(
        block, AXES, route(lambda lat, lon, lats, lons: (lat ^ lat_bits, lon ^ lon_bits))
    )


def outer_move(lat, lon, lats, lons):
    if lat == 0 or lat == lats - 1:
        return lat, (lon + lons // 2) % lons
    return (lat - 1 if lat % 2 == 0 else lat + 1), lon


def along_move(lat, lon, lats, lons):
    return lat, (lon + 2 if lon % 2 else lon - 2) % lons


def across_move(lat, lon, lats, lons):
    return lat, (lon + 1 if lon % 2 else lon - 1) % lons


def lane_of(value):
    return lax.broadcasted_iota(jnp.int32, value.shape, 1)


def turned(value, lanes):
    return pltpu.roll(value, lanes, 1)


def put(refs, odd, at, low, high):
    wide = low.shape[1]
    low, high = low.astype(jnp.bfloat16), high.astype(jnp.bfloat16)
    refs[0][:, at : at + wide] = jnp.where(odd == 1, high, low)
    refs[1][:, at : at + wide] = jnp.where(odd == 1, low, high)


def put_main(refs, odd, at, value, main):
    put(refs, odd, at, value[:, :main], value[:, main : 2 * main])


def split_of(value, main):
    return value[:, 2 * main : 2 * main + LANES].astype(jnp.float32)


def put_pair(refs, odd, at, first, second, main):
    put_main(refs, odd, at, first, main)
    put_main(refs, odd, at + main, second, main)
    first, second = split_of(first, main), split_of(second, main)
    front = lane_of(first) < HALF
    low = jnp.where(front, first, turned(second, HALF))
    high = jnp.where(front, turned(first, HALF), second)
    put(refs, odd, at + 2 * main, low, high)


def spare_of(tile, values, main, start):
    lane = lane_of(tile)
    for at, value in enumerate(values):
        last = value[:, 2 * main + LANES :].astype(jnp.float32)
        tile = jnp.where(lane == start + at, jnp.broadcast_to(last, tile.shape), tile)
    return tile


def weight_kernel(main, w_ref, own_ref, pair_ref):
    odd = lax.axis_index("lon") % 2
    refs = own_ref, pair_ref
    bases = w_ref.shape[0]
    values = [w_ref[k] for k in range(bases)]
    for k in range(0, bases - 1, 2):
        put_pair(refs, odd, k // 2 * (2 * main + LANES), values[k], values[k + 1], main)
    at = bases // 2 * (2 * main + LANES)
    put_main(refs, odd, at, values[-1], main)
    tile = split_of(values[-1], main)
    front = lane_of(tile) < HALF
    low, high = jnp.where(front, tile, 0.0), jnp.where(front, turned(tile, HALF), 0.0)
    put(refs, odd, at + main, low, spare_of(high, values, main, HALF))


def edge_kernel(x_ref, outer_ref, held_ref):
    radius = outer_ref.shape[0]
    lower = lax.axis_index("lat") % 2
    outer_ref[...] = jnp.where(lower == 1, x_ref[-radius:], x_ref[:radius])
    held_ref[...] = x_ref[...]


def start_kernel(main, w_ref, x_ref, own_ref, pair_ref, outer_ref, held_ref):
    weight_kernel(main, w_ref, own_ref, pair_ref)
    edge_kernel(x_ref, outer_ref, held_ref)


def strip_kernel(main, x_ref, outer_ref, mine_ref, other_ref, rows_ref):
    lat, odd = lax.axis_index("lat"), lax.axis_index("lon") % 2
    pole = (lat == 0) | (lat == lax.axis_size("lat") - 1)
    radius, rows = outer_ref.shape[0], x_ref.shape[0]
    rows_ref[pl.ds((1 - lat % 2) * radius, rows)] = x_ref[...]
    for r in range(radius):
        rows_ref[lat % 2 * rows + r] = outer_ref[jnp.where(pole, radius - 1 - r, r)]
    refs = mine_ref, other_ref
    count = rows_ref.shape[0]
    values = [rows_ref[r] for r in range(count)]
    for r in range(count // 2):
        at = r * (2 * main + LANES)
        put_pair(refs, odd, at, values[r], values[r + count // 2], main)
    none = jnp.zeros((x_ref.shape[1], LANES), jnp.float32)
    put(refs, odd, count // 2 * (2 * main + LANES), none, spare_of(none, values, main, 0))


def join_kernel(mine_ref, other_ref, out_ref):
    odd = lax.axis_index("lon") % 2
    share = mine_ref.shape[0]
    low, high = mine_ref[...], other_ref[...]
    out_ref[:share] = jnp.where(odd == 1, high, low)
    out_ref[share:] = jnp.where(odd == 1, low, high)


def copy_kernel(source_ref, out_ref):
    out_ref[...] = source_ref[...]


def stack_kernel(*refs):
    for at, ref in enumerate(refs[:-1]):
        refs[-1][at] = ref[...]


def band_kernel(reach, f_ref, w_ref, band_ref, row_ref):
    bases, span, rows, taps = f_ref.shape
    columns = band_ref.shape[1] // (2 * bases)
    pitch = columns + taps - 1
    wide = band_ref.shape[2]
    offset = jnp.abs(lax.broadcasted_iota(jnp.int32, (rows, taps), 1) - reach)
    row_ref[...] = jnp.zeros_like(row_ref)
    for d in range(span):
        inside = offset <= w_ref[:, d : d + 1]
        for k in range(bases):
            tap = jnp.where(inside, f_ref[k, d].astype(jnp.float32), 0.0)
            row_ref[k, :, d * pitch : d * pitch + taps] = tap

    def one_pair(pair, _):
        for e in range(2):
            for k in range(bases):
                same = jnp.broadcast_to(row_ref[k, pl.ds(2 * pair + e, 1), :], (columns, wide))
                band = pltpu.roll(same, e * pitch, 1, stride=1, stride_axis=0)
                at = (e * bases + k) * columns
                band_ref[pair, at : at + columns, :] = band.astype(jnp.bfloat16)
        return 0

    lax.fori_loop(0, rows // 2, one_pair, 0)


def unpack(source_ref, slab_ref, slot, main):
    count = slab_ref.shape[0]
    wide = 2 * main + LANES
    spare = source_ref[:, count // 2 * wide :].astype(jnp.float32)
    lane = lane_of(spare)
    for r in range(count // 2):
        tile = source_ref[:, r * wide + 2 * main : (r + 1) * wide].astype(jnp.float32)
        for row, third in ((r, tile), (r + count // 2, turned(tile, HALF))):
            at = r * wide + (main if row > r else 0)
            slab_ref[row, slot, :, :main] = source_ref[:, at : at + main]
            last = turned(spare, (HALF - row) % LANES)
            third = jnp.where(lane == HALF, last, third)
            slab_ref[row, slot, :, main:] = third.astype(jnp.bfloat16)


def slab_kernel(mine_ref, pair_ref, along_ref, across_ref, slab_ref, inner_ref):
    odd = lax.axis_index("lon") % 2
    main = slab_ref.shape[3] - LANES
    unpack(mine_ref, slab_ref, 1 + odd, main)
    unpack(pair_ref, slab_ref, 2 - odd, main)
    unpack(along_ref, slab_ref, 3 * (1 - odd), main)
    unpack(across_ref, slab_ref, 3 * odd, main)
    radius = inner_ref.shape[0]
    start = (1 - lax.axis_index("lat") % 2) * (slab_ref.shape[0] - radius)
    inner_ref[...] = slab_ref[pl.ds(start, radius)]


def feature_kernel(span, band_ref, rows_ref, inner_ref, out_ref, slab_ref):
    lower = lax.axis_index("lat") % 2
    held, radius = rows_ref.shape[0], inner_ref.shape[0]
    slab_ref[pl.ds(lower * radius, held)] = rows_ref[...]
    slab_ref[pl.ds((1 - lower) * held, radius)] = inner_ref[...]
    strips, rows, columns, _ = out_ref.shape
    half = slab_ref.shape[3]
    main = half - LANES
    bases = band_ref.shape[1] // (2 * columns)
    depth = (span + 1) * 3 * columns
    wide = 2 * main + LANES

    def one_pair(pair, _):
        band = band_ref[pair][:, :depth]
        source = [
            slab_ref[pl.ds(2 * pair, span + 1), strip : strip + 3].reshape(depth, half)
            for strip in range(strips)
        ]
        summed = jnp.dot(
            band, jnp.concatenate(source, axis=1), preferred_element_type=jnp.float32
        )
        for e in range(2):
            for strip in range(strips):

                def save(at, value):
                    out_ref[strip, 2 * pair + e, :, at : at + value.shape[1]] = value.astype(
                        jnp.bfloat16
                    )

                parts = []
                for k in range(bases):
                    at = (e * bases + k) * columns
                    parts.append(summed[at : at + columns, strip * half : (strip + 1) * half])
                lane = lane_of(parts[0][:, main:])
                for k, part in enumerate(parts):
                    save(k // 2 * wide + k % 2 * main, part[:, :main])
                for k in range(0, bases - 1, 2):
                    second = turned(parts[k + 1][:, main:], HALF)
                    save(k // 2 * wide + 2 * main, jnp.where(lane < HALF, parts[k][:, main:], second))
                tile = parts[-1][:, main:]
                for k in range(bases):
                    tile = jnp.where(lane == HALF + k, turned(parts[k][:, main:], k), tile)
                save(bases // 2 * wide + main, tile)
        return 0

    lax.fori_loop(0, rows // 2, one_pair, 0)


def product(feature_ref, strip, weight):
    return lax.dot_general(
        feature_ref[strip], weight, (((1,), (1,)), ((), ())), preferred_element_type=jnp.float32
    )


def partner_mix_kernel(sources, feature_ref, *refs):
    piece_refs = refs[: len(sources)]
    send_ref, weight_ref = refs[len(sources) :]
    lat, lon = lax.axis_index("lat"), lax.axis_index("lon")
    masks = lax.axis_size("lon") // 2
    if sum(len(keys) for _, keys in sources) < weight_ref.shape[0]:
        weight_ref[...] = jnp.zeros_like(weight_ref)
    for (core, keys), ref in zip(sources, piece_refs):
        for at, (low, mask) in enumerate(keys):
            row = 2 * ((lat // 2) ^ low) + (lat % 2 ^ core)
            weight_ref[row * masks + ((lon // 2) ^ mask)] = ref[at]
    weight = weight_ref[...].reshape(send_ref.shape[1], weight_ref.shape[2])
    send_ref[...] = product(feature_ref, 1 - lon % 2, weight).astype(send_ref.dtype)


def own_mix_kernel(feature_ref, weight_ref, keep_ref):
    weight = weight_ref[...].reshape(keep_ref.shape[1], weight_ref.shape[2])
    keep_ref[...] = product(feature_ref, lax.axis_index("lon") % 2, weight)


def rest_kernel(own, feature_ref, own_ref, crossed_ref, sum_ref):
    odd = lax.axis_index("lon") % 2
    weight = jnp.concatenate([own_ref[0], crossed_ref[0]], axis=0)
    count = sum_ref.shape[0]
    total = product(feature_ref, odd if own else 1 - odd, weight)
    sum_ref[...] = jnp.concatenate([total[:count], total[count:]], axis=1).astype(sum_ref.dtype)


def finish_kernel(last, block, keep_ref, got_ref, keep2_ref, got2_ref, bias_ref, out_ref):
    lat, lon = lax.axis_index("lat"), lax.axis_index("lon")
    wide = out_ref.shape[1] // 2

    def save(rows, at, total):
        total += bias_ref[:, at]
        grown = 0.5 * total * (1.0 + lax.erf(total * 0.5**0.5))
        out_ref[rows, at] = grown.astype(out_ref.dtype)

    at = pl.ds(pl.multiple_of(lat // 2 * wide, LANES), wide)
    save(slice(None), at, keep_ref[:, at] + got_ref[:, at].astype(jnp.float32))
    rest = keep2_ref[...] + got2_ref[...].astype(jnp.float32)
    count = rest.shape[0]
    lane = lane_of(rest)
    start = ((lon // 2) ^ last) * block
    inside = (lane >= start) & (lane < start + block)
    for crossed in range(2):
        tile = (1 - lat // 2) * 2 + (lat % 2 ^ crossed)
        at = pl.ds(pl.multiple_of(tile * LANES, LANES), LANES)
        for part in range(2):
            rows = slice(part * count, (part + 1) * count)
            held = part * (2 * block) + crossed * block
            moved = pltpu.roll(rest, lax.rem(start - held + LANES, LANES), 1)
            total = keep_ref[rows, at] + got_ref[rows, at].astype(jnp.float32)
            save(rows, at, jnp.where(inside, moved, total))


def body(latent, filters, widths, mix_weight, mix_bias):
    lats, lons = lax.axis_size("lat"), lax.axis_size("lon")
    rows, columns, channels = latent.shape
    bases, _, span, taps = filters.shape
    radius, reach = span // 2, taps // 2
    assert reach == columns and rows % 2 == lats % 2 == lons % 2 == 0
    main = channels // (2 * LANES) * LANES
    assert channels == 2 * main + LANES + 1 and bases % 2 == 1
    assert bases <= HALF and rows + 2 * radius <= LANES
    half, packed = main + LANES, 2 * main + LANES
    out_columns, share = mix_bias.shape[0], mix_weight.shape[2]
    depth = bases // 2 * packed + half

    edge, halves = shape((radius, columns, channels)), shape((share, depth))
    weights = jnp.transpose(mix_weight, (0, 2, 1))
    own_weight, pair_weight = call(
        functools.partial(weight_kernel, main), (halves, halves), [], weights
    )
    outer, held_latent = call(edge_kernel, (edge, shape(latent.shape)), [], latent)
    got_weight = swap(pair_weight, 0, 1)
    from_outer = lax.ppermute(outer, AXES, route(outer_move))
    block = shape((2 * share, depth))
    first = call(join_kernel, block, [], own_weight, got_weight)

    lon_masks, lat_masks = lons // 2, lats // 2
    steps = [1 << at for at in range(lat_masks.bit_length() - 1)]
    blocks = {(0, 0): first}
    bit = lon_masks // 2
    while bit:
        for low, mask in list(blocks):
            blocks[low, mask ^ bit] = swap(blocks[low, mask], 0, 2 * bit)
        bit //= 2
    order = [mask for _, mask in blocks]
    last = order[-1]
    count = rows + radius
    strip = shape((columns, count // 2 * packed + LANES))

    def cross(masks):
        for bit in steps:
            for low in range(bit):
                for mask in masks:
                    blocks[low ^ bit, mask] = swap(blocks[low, mask], 2 * bit, 0)

    cross(order[:1])
    mine, other = call(
        functools.partial(strip_kernel, main),
        (strip, strip),
        [pltpu.VMEM((count, columns, channels), jnp.bfloat16)],
        held_latent,
        from_outer,
    )
    for mask in order[1:-1]:
        blocks[0, mask] = call(copy_kernel, block, [], blocks[0, mask], after=(mine,))
    cross(order[1:-1])
    pair_strip = swap(other, 0, 1)
    along = lax.ppermute(mine, AXES, route(along_move))
    across = lax.ppermute(other, AXES, route(across_move))
    deep = -(-(span + 1) * 3 * columns // LANES) * LANES
    band = call(
        functools.partial(band_kernel, reach),
        shape((rows // 2, 2 * bases * columns, deep)),
        [pltpu.VMEM((bases, rows, deep), jnp.float32)],
        jnp.transpose(filters, (0, 2, 1, 3)),
        widths,
        after=(pair_strip,),
    )
    slab, inner = call(
        slab_kernel,
        (shape((count, 4, columns, half)), shape((radius, 4, columns, half))),
        [],
        mine,
        pair_strip,
        along,
        across,
    )
    from_inner = swap(inner, 1, 0)

    features = call(
        functools.partial(feature_kernel, span),
        shape((2, rows, columns, depth)),
        [pltpu.VMEM((rows + 2 * radius, 4, columns, half), jnp.bfloat16)],
        band,
        slab,
        from_inner,
    )
    features = features.reshape(2, rows * columns, depth)
    met = [value for key, value in blocks.items() if key != (0, last)]
    blocks[0, last] = call(
        copy_kernel, block, [], blocks[0, last], after=(*met, features)
    )
    cross(order[-1:])
    points = rows * columns

    def stacked(keys, after):
        values = [blocks[key] for key in keys]
        piece = call(
            stack_kernel, shape((len(keys),) + block.shape), [], *values, after=after
        )
        return [piece, swap(piece, 1, 0)]

    apart = lat_masks == 2 and 8 * share == LANES == lon_masks * 2 * share and points % 2 == 0
    early = [key for key in blocks if key[1] == 0 or (key[0] == 0 and key[1] != last)]
    late = [key for key in blocks if key not in early and not (apart and key == (1, last))]
    sources, pieces = [], []
    for keys, after in ((early, (slab,)), (late, (features,))):
        if keys:
            sources += [(core, keys) for core in range(2)]
            pieces += stacked(keys, after)
    send, weight = call(
        functools.partial(partner_mix_kernel, sources),
        (shape((points, out_columns)), shape((lats * lon_masks,) + block.shape)),
        [],
        features,
        *pieces,
    )
    got = swap(send, 0, 1)
    sums = shape((points, out_columns), jnp.float32)
    if not apart:
        keep = call(own_mix_kernel, sums, [], features, weight)
        total = (keep + got.astype(jnp.float32)).reshape(rows, columns, out_columns) + mix_bias
        return jax.nn.gelu(total, approximate=False).astype(jnp.bfloat16)
    rest, pieces = (points // 2, LANES), stacked([(1, last)], (send,))
    rest_send = call(
        functools.partial(rest_kernel, False), shape(rest), [], features, *pieces
    )
    rest_got = swap(rest_send, 0, 1)
    keep = call(own_mix_kernel, sums, [], features, weight, after=(rest_send,))
    rest_keep = call(
        functools.partial(rest_kernel, True),
        shape(rest, jnp.float32),
        [],
        features,
        *pieces,
        after=(rest_send,),
    )
    out = call(
        functools.partial(finish_kernel, last, 2 * share),
        shape((points, out_columns)),
        [],
        keep,
        got,
        rest_keep,
        rest_got,
        mix_bias[None],
    )
    return out.reshape(rows, columns, out_columns)


def solution(mesh):
    placed = (
        P("lat", "lon", None),
        P(None, "lat", None, None),
        P("lat", None),
        P(None, None, ("lat", "lon")),
        P(),
    )
    return jax.shard_map(
        body, mesh=mesh, in_specs=placed, out_specs=P("lat", "lon", None), check_vma=False
    )
```

```python
import functools

import jax
import jax.numpy as jnp
from jax import lax
from jax.experimental import pallas as pl
from jax.experimental.pallas import tpu as pltpu
from jax.sharding import PartitionSpec as P


AXES = ("lat", "lon")
LANES = 128
HALF = LANES // 2
VMEM_BYTES = 20 * 1024 * 1024


def call(kernel, outs, scratch, *args, after=()):
    held = pl.BlockSpec(memory_space=pltpu.VMEM)
    count = len(args)

    def ordered(*refs):
        kernel(*refs[:count], *refs[count + len(after) :])

    return pl.pallas_call(
        ordered,
        out_shape=outs,
        in_specs=[held] * count + [pl.BlockSpec(memory_space=pl.ANY)] * len(after),
        out_specs=jax.tree.map(lambda _: held, outs),
        scratch_shapes=scratch,
        compiler_params=pltpu.CompilerParams(vmem_limit_bytes=VMEM_BYTES),
    )(*args, *after)


def shape(dims, dtype=jnp.bfloat16):
    return jax.ShapeDtypeStruct(dims, dtype)


def route(move):
    lats, lons = lax.axis_size("lat"), lax.axis_size("lon")
    pairs = []
    for lat in range(lats):
        for lon in range(lons):
            to_lat, to_lon = move(lat, lon, lats, lons)
            pairs.append((lat * lons + lon, to_lat * lons + to_lon))
    return pairs


def swap(block, lat_bits, lon_bits):
    return lax.ppermute(
        block, AXES, route(lambda lat, lon, lats, lons: (lat ^ lat_bits, lon ^ lon_bits))
    )


def outer_move(lat, lon, lats, lons):
    if lat == 0 or lat == lats - 1:
        return lat, (lon + lons // 2) % lons
    return (lat - 1 if lat % 2 == 0 else lat + 1), lon


def along_move(lat, lon, lats, lons):
    return lat, (lon + 2 if lon % 2 else lon - 2) % lons


def across_move(lat, lon, lats, lons):
    return lat, (lon + 1 if lon % 2 else lon - 1) % lons


def lane_of(value):
    return lax.broadcasted_iota(jnp.int32, value.shape, 1)


def turned(value, lanes):
    return pltpu.roll(value, lanes, 1)


def put(refs, odd, at, low, high):
    wide = low.shape[1]
    low, high = low.astype(jnp.bfloat16), high.astype(jnp.bfloat16)
    refs[0][:, at : at + wide] = jnp.where(odd == 1, high, low)
    refs[1][:, at : at + wide] = jnp.where(odd == 1, low, high)


def put_main(refs, odd, at, value, main):
    put(refs, odd, at, value[:, :main], value[:, main : 2 * main])


def split_of(value, main):
    return value[:, 2 * main : 2 * main + LANES].astype(jnp.float32)


def put_pair(refs, odd, at, first, second, main):
    put_main(refs, odd, at, first, main)
    put_main(refs, odd, at + main, second, main)
    first, second = split_of(first, main), split_of(second, main)
    front = lane_of(first) < HALF
    low = jnp.where(front, first, turned(second, HALF))
    high = jnp.where(front, turned(first, HALF), second)
    put(refs, odd, at + 2 * main, low, high)


def spare_of(tile, values, main, start):
    lane = lane_of(tile)
    for at, value in enumerate(values):
        last = value[:, 2 * main + LANES :].astype(jnp.float32)
        tile = jnp.where(lane == start + at, jnp.broadcast_to(last, tile.shape), tile)
    return tile


def weight_kernel(main, w_ref, own_ref, pair_ref):
    odd = lax.axis_index("lon") % 2
    refs = own_ref, pair_ref
    bases = w_ref.shape[0]
    values = [w_ref[k] for k in range(bases)]
    for k in range(0, bases - 1, 2):
        put_pair(refs, odd, k // 2 * (2 * main + LANES), values[k], values[k + 1], main)
    at = bases // 2 * (2 * main + LANES)
    put_main(refs, odd, at, values[-1], main)
    tile = split_of(values[-1], main)
    front = lane_of(tile) < HALF
    low, high = jnp.where(front, tile, 0.0), jnp.where(front, turned(tile, HALF), 0.0)
    put(refs, odd, at + main, low, spare_of(high, values, main, HALF))


def edge_kernel(x_ref, outer_ref, held_ref):
    radius = outer_ref.shape[0]
    lower = lax.axis_index("lat") % 2
    outer_ref[...] = jnp.where(lower == 1, x_ref[-radius:], x_ref[:radius])
    held_ref[...] = x_ref[...]


def start_kernel(main, w_ref, x_ref, own_ref, pair_ref, outer_ref, held_ref):
    weight_kernel(main, w_ref, own_ref, pair_ref)
    edge_kernel(x_ref, outer_ref, held_ref)


def strip_kernel(main, x_ref, outer_ref, mine_ref, other_ref, rows_ref):
    lat, odd = lax.axis_index("lat"), lax.axis_index("lon") % 2
    pole = (lat == 0) | (lat == lax.axis_size("lat") - 1)
    radius, rows = outer_ref.shape[0], x_ref.shape[0]
    rows_ref[pl.ds((1 - lat % 2) * radius, rows)] = x_ref[...]
    for r in range(radius):
        rows_ref[lat % 2 * rows + r] = outer_ref[jnp.where(pole, radius - 1 - r, r)]
    refs = mine_ref, other_ref
    count = rows_ref.shape[0]
    values = [rows_ref[r] for r in range(count)]
    for r in range(count // 2):
        at = r * (2 * main + LANES)
        put_pair(refs, odd, at, values[r], values[r + count // 2], main)
    none = jnp.zeros((x_ref.shape[1], LANES), jnp.float32)
    put(refs, odd, count // 2 * (2 * main + LANES), none, spare_of(none, values, main, 0))


def join_kernel(mine_ref, other_ref, out_ref):
    odd = lax.axis_index("lon") % 2
    share = mine_ref.shape[0]
    low, high = mine_ref[...], other_ref[...]
    out_ref[:share] = jnp.where(odd == 1, high, low)
    out_ref[share:] = jnp.where(odd == 1, low, high)


def copy_kernel(source_ref, out_ref):
    out_ref[...] = source_ref[...]


def stack_kernel(*refs):
    for at, ref in enumerate(refs[:-1]):
        refs[-1][at] = ref[...]


def band_kernel(reach, f_ref, w_ref, band_ref, row_ref):
    bases, span, rows, taps = f_ref.shape
    columns = band_ref.shape[1] // (2 * bases)
    pitch = columns + taps - 1
    wide = band_ref.shape[2]
    offset = jnp.abs(lax.broadcasted_iota(jnp.int32, (rows, taps), 1) - reach)
    row_ref[...] = jnp.zeros_like(row_ref)
    for d in range(span):
        inside = offset <= w_ref[:, d : d + 1]
        for k in range(bases):
            tap = jnp.where(inside, f_ref[k, d].astype(jnp.float32), 0.0)
            row_ref[k, :, d * pitch : d * pitch + taps] = tap

    def one_pair(pair, _):
        for e in range(2):
            for k in range(bases):
                same = jnp.broadcast_to(row_ref[k, pl.ds(2 * pair + e, 1), :], (columns, wide))
                band = pltpu.roll(same, e * pitch, 1, stride=1, stride_axis=0)
                at = (e * bases + k) * columns
                band_ref[pair, at : at + columns, :] = band.astype(jnp.bfloat16)
        return 0

    lax.fori_loop(0, rows // 2, one_pair, 0)


def unpack(source_ref, slab_ref, slot, main):
    count = slab_ref.shape[0]
    wide = 2 * main + LANES
    spare = source_ref[:, count // 2 * wide :].astype(jnp.float32)
    lane = lane_of(spare)
    for r in range(count // 2):
        tile = source_ref[:, r * wide + 2 * main : (r + 1) * wide].astype(jnp.float32)
        for row, third in ((r, tile), (r + count // 2, turned(tile, HALF))):
            at = r * wide + (main if row > r else 0)
            slab_ref[row, slot, :, :main] = source_ref[:, at : at + main]
            last = turned(spare, (HALF - row) % LANES)
            third = jnp.where(lane == HALF, last, third)
            slab_ref[row, slot, :, main:] = third.astype(jnp.bfloat16)


def slab_kernel(mine_ref, pair_ref, along_ref, across_ref, slab_ref, inner_ref):
    odd = lax.axis_index("lon") % 2
    main = slab_ref.shape[3] - LANES
    unpack(mine_ref, slab_ref, 1 + odd, main)
    unpack(pair_ref, slab_ref, 2 - odd, main)
    unpack(along_ref, slab_ref, 3 * (1 - odd), main)
    unpack(across_ref, slab_ref, 3 * odd, main)
    radius = inner_ref.shape[0]
    start = (1 - lax.axis_index("lat") % 2) * (slab_ref.shape[0] - radius)
    inner_ref[...] = slab_ref[pl.ds(start, radius)]


def feature_kernel(span, band_ref, rows_ref, inner_ref, out_ref, slab_ref):
    lower = lax.axis_index("lat") % 2
    held, radius = rows_ref.shape[0], inner_ref.shape[0]
    slab_ref[pl.ds(lower * radius, held)] = rows_ref[...]
    slab_ref[pl.ds((1 - lower) * held, radius)] = inner_ref[...]
    strips, rows, columns, _ = out_ref.shape
    half = slab_ref.shape[3]
    main = half - LANES
    bases = band_ref.shape[1] // (2 * columns)
    depth = (span + 1) * 3 * columns
    wide = 2 * main + LANES

    def one_pair(pair, _):
        band = band_ref[pair][:, :depth]
        source = [
            slab_ref[pl.ds(2 * pair, span + 1), strip : strip + 3].reshape(depth, half)
            for strip in range(strips)
        ]
        summed = jnp.dot(
            band, jnp.concatenate(source, axis=1), preferred_element_type=jnp.float32
        )
        for e in range(2):
            for strip in range(strips):

                def save(at, value):
                    out_ref[strip, 2 * pair + e, :, at : at + value.shape[1]] = value.astype(
                        jnp.bfloat16
                    )

                parts = []
                for k in range(bases):
                    at = (e * bases + k) * columns
                    parts.append(summed[at : at + columns, strip * half : (strip + 1) * half])
                lane = lane_of(parts[0][:, main:])
                for k, part in enumerate(parts):
                    save(k // 2 * wide + k % 2 * main, part[:, :main])
                for k in range(0, bases - 1, 2):
                    second = turned(parts[k + 1][:, main:], HALF)
                    save(k // 2 * wide + 2 * main, jnp.where(lane < HALF, parts[k][:, main:], second))
                tile = parts[-1][:, main:]
                for k in range(bases):
                    tile = jnp.where(lane == HALF + k, turned(parts[k][:, main:], k), tile)
                save(bases // 2 * wide + main, tile)
        return 0

    lax.fori_loop(0, rows // 2, one_pair, 0)


def product(feature_ref, strip, weight):
    return lax.dot_general(
        feature_ref[strip], weight, (((1,), (1,)), ((), ())), preferred_element_type=jnp.float32
    )


def partner_mix_kernel(sources, feature_ref, *refs):
    piece_refs = refs[: len(sources)]
    send_ref, weight_ref = refs[len(sources) :]
    lat, lon = lax.axis_index("lat"), lax.axis_index("lon")
    masks = lax.axis_size("lon") // 2
    if sum(len(held) for _, _, held in sources) < weight_ref.shape[0]:
        weight_ref[...] = jnp.zeros_like(weight_ref)
    for (core, low, held), ref in zip(sources, piece_refs):
        row = 2 * ((lat // 2) ^ low) + (lat % 2 ^ core)
        for at, mask in enumerate(held):
            weight_ref[row * masks + ((lon // 2) ^ mask)] = ref[at]
    weight = weight_ref[...].reshape(send_ref.shape[1], weight_ref.shape[2])
    send_ref[...] = product(feature_ref, 1 - lon % 2, weight).astype(send_ref.dtype)


def own_mix_kernel(feature_ref, weight_ref, keep_ref):
    weight = weight_ref[...].reshape(keep_ref.shape[1], weight_ref.shape[2])
    keep_ref[...] = product(feature_ref, lax.axis_index("lon") % 2, weight)


def rest_kernel(own, feature_ref, own_ref, crossed_ref, sum_ref):
    odd = lax.axis_index("lon") % 2
    weight = jnp.concatenate([own_ref[0], crossed_ref[0]], axis=0)
    count = sum_ref.shape[0]
    total = product(feature_ref, odd if own else 1 - odd, weight)
    sum_ref[...] = jnp.concatenate([total[:count], total[count:]], axis=1).astype(sum_ref.dtype)


def grown(total):
    return 0.5 * total * (1.0 + lax.erf(total * 0.5**0.5))


def main_kernel(keep_ref, got_ref, bias_ref, out_ref):
    total = keep_ref[...] + got_ref[...].astype(jnp.float32) + bias_ref[...]
    out_ref[...] = grown(total).astype(out_ref.dtype)


def finish_kernel(last, block, main_ref, keep_ref, got_ref, bias_ref, out_ref):
    lat, lon = lax.axis_index("lat"), lax.axis_index("lon")
    out_ref[...] = main_ref[...]
    rest = keep_ref[...] + got_ref[...].astype(jnp.float32)
    count = rest.shape[0]
    lane = lane_of(rest)
    start = ((lon // 2) ^ last) * block
    inside = (lane >= start) & (lane < start + block)
    spots = []
    for crossed in range(2):
        tile = (1 - lat // 2) * 2 + (lat % 2 ^ crossed)
        at = pl.ds(pl.multiple_of(tile * LANES, LANES), LANES)
        spots += [(at, part, part * (2 * block) + crossed * block) for part in range(2)]
    bias = jnp.zeros((8, LANES), jnp.float32)
    narrow = lane_of(bias)
    for at, _, held in spots:
        moved = jnp.broadcast_to(bias_ref[:, at], bias.shape)
        moved = pltpu.roll(moved, lax.rem(held - start + LANES, LANES), 1)
        bias = jnp.where((narrow >= held) & (narrow < held + block), moved, bias)
    value = grown(rest + bias[:1])
    for at, part, held in spots:
        rows = slice(part * count, (part + 1) * count)
        moved = pltpu.roll(value, lax.rem(start - held + LANES, LANES), 1)
        merged = jnp.where(inside, moved, main_ref[rows, at].astype(jnp.float32))
        out_ref[rows, at] = merged.astype(out_ref.dtype)


def body(latent, filters, widths, mix_weight, mix_bias):
    lats, lons = lax.axis_size("lat"), lax.axis_size("lon")
    rows, columns, channels = latent.shape
    bases, _, span, taps = filters.shape
    radius, reach = span // 2, taps // 2
    assert reach == columns and rows % 2 == lats % 2 == lons % 2 == 0
    main = channels // (2 * LANES) * LANES
    assert channels == 2 * main + LANES + 1 and bases % 2 == 1
    assert bases <= HALF and rows + 2 * radius <= LANES
    half, packed = main + LANES, 2 * main + LANES
    out_columns, share = mix_bias.shape[0], mix_weight.shape[2]
    depth = bases // 2 * packed + half

    edge, halves = shape((radius, columns, channels)), shape((share, depth))
    weights = jnp.transpose(mix_weight, (0, 2, 1))
    own_weight, pair_weight = call(
        functools.partial(weight_kernel, main), (halves, halves), [], weights
    )
    outer, held_latent = call(edge_kernel, (edge, shape(latent.shape)), [], latent)
    got_weight = swap(pair_weight, 0, 1)
    from_outer = lax.ppermute(outer, AXES, route(outer_move))
    block = shape((2 * share, depth))
    first = call(join_kernel, block, [], own_weight, got_weight)

    lon_masks, lat_masks = lons // 2, lats // 2
    steps = [1 << at for at in range(lat_masks.bit_length() - 1)]
    blocks = {(0, 0): first}
    bit = lon_masks // 2
    while bit:
        for low, mask in list(blocks):
            blocks[low, mask ^ bit] = swap(blocks[low, mask], 0, 2 * bit)
        bit //= 2
    order = [mask for _, mask in blocks]
    last = order[-1]
    count = rows + radius
    strip = shape((columns, count // 2 * packed + LANES))

    def cross(masks):
        for bit in steps:
            for low in range(bit):
                for mask in masks:
                    blocks[low ^ bit, mask] = swap(blocks[low, mask], 2 * bit, 0)

    cross(order[:1])
    mine, other = call(
        functools.partial(strip_kernel, main),
        (strip, strip),
        [pltpu.VMEM((count, columns, channels), jnp.bfloat16)],
        held_latent,
        from_outer,
    )
    for mask in order[1:-1]:
        blocks[0, mask] = call(copy_kernel, block, [], blocks[0, mask], after=(mine,))
    cross(order[1:-1])
    pair_strip = swap(other, 0, 1)
    along = lax.ppermute(mine, AXES, route(along_move))
    across = lax.ppermute(other, AXES, route(across_move))
    deep = -(-(span + 1) * 3 * columns // LANES) * LANES
    band = call(
        functools.partial(band_kernel, reach),
        shape((rows // 2, 2 * bases * columns, deep)),
        [pltpu.VMEM((bases, rows, deep), jnp.float32)],
        jnp.transpose(filters, (0, 2, 1, 3)),
        widths,
        after=(pair_strip,),
    )
    slab, inner = call(
        slab_kernel,
        (shape((count, 4, columns, half)), shape((radius, 4, columns, half))),
        [],
        mine,
        pair_strip,
        along,
        across,
    )
    from_inner = swap(inner, 1, 0)

    features = call(
        functools.partial(feature_kernel, span),
        shape((2, rows, columns, depth)),
        [pltpu.VMEM((rows + 2 * radius, 4, columns, half), jnp.bfloat16)],
        band,
        slab,
        from_inner,
    )
    features = features.reshape(2, rows * columns, depth)
    met = [value for key, value in blocks.items() if key != (0, last)]
    blocks[0, last] = call(
        copy_kernel, block, [], blocks[0, last], after=(*met, features)
    )
    cross(order[-1:])
    points = rows * columns

    def stacked(low, held, after):
        piece = call(
            stack_kernel,
            shape((len(held),) + block.shape),
            [],
            *[blocks[low, mask] for mask in held],
            after=after,
        )
        return [piece, swap(piece, 1, 0)]

    apart = lat_masks == 2 and 8 * share == LANES == lon_masks * 2 * share and points % 2 == 0
    sources, pieces = [], []
    for low in range(lat_masks):
        held = order[:-1] if low and apart else order
        sources += [(core, low, held) for core in range(2)]
        pieces += stacked(low, held, (blocks[0, last],) if low == 0 else (blocks[0, last],))
    send, weight = call(
        functools.partial(partner_mix_kernel, sources),
        (shape((points, out_columns)), shape((lats * lon_masks,) + block.shape)),
        [],
        features,
        *pieces,
    )
    got = swap(send, 0, 1)
    sums = shape((points, out_columns), jnp.float32)
    if not apart:
        keep = call(own_mix_kernel, sums, [], features, weight)
        total = (keep + got.astype(jnp.float32)).reshape(rows, columns, out_columns) + mix_bias
        return jax.nn.gelu(total, approximate=False).astype(jnp.bfloat16)
    rest, pieces = (points // 2, LANES), stacked(1, order[-1:], (send,))
    rest_send = call(
        functools.partial(rest_kernel, False), shape(rest), [], features, *pieces
    )
    rest_got = swap(rest_send, 0, 1)
    keep = call(own_mix_kernel, sums, [], features, weight, after=(rest_send,))
    rest_keep = call(
        functools.partial(rest_kernel, True),
        shape(rest, jnp.float32),
        [],
        features,
        *pieces,
        after=(rest_send,),
    )
    done = call(
        main_kernel, shape((points, out_columns)), [], keep, got, mix_bias[None]
    )
    out = call(
        functools.partial(finish_kernel, last, 2 * share),
        shape((points, out_columns)),
        [],
        done,
        rest_keep,
        rest_got,
        mix_bias[None],
    )
    return out.reshape(rows, columns, out_columns)


def solution(mesh):
    placed = (
        P("lat", "lon", None),
        P(None, "lat", None, None),
        P("lat", None),
        P(None, None, ("lat", "lon")),
        P(),
    )
    return jax.shard_map(
        body, mesh=mesh, in_specs=placed, out_specs=P("lat", "lon", None), check_vma=False
    )
```

```python
import functools

import jax
import jax.numpy as jnp
from jax import lax
from jax.experimental import pallas as pl
from jax.experimental.pallas import tpu as pltpu
from jax.sharding import PartitionSpec as P


AXES = ("lat", "lon")
LANES = 128
HALF = LANES // 2
VMEM_BYTES = 20 * 1024 * 1024


def call(kernel, outs, scratch, *args, after=()):
    held = pl.BlockSpec(memory_space=pltpu.VMEM)
    count = len(args)

    def ordered(*refs):
        kernel(*refs[:count], *refs[count + len(after) :])

    return pl.pallas_call(
        ordered,
        out_shape=outs,
        in_specs=[held] * count + [pl.BlockSpec(memory_space=pl.ANY)] * len(after),
        out_specs=jax.tree.map(lambda _: held, outs),
        scratch_shapes=scratch,
        compiler_params=pltpu.CompilerParams(vmem_limit_bytes=VMEM_BYTES),
    )(*args, *after)


def shape(dims, dtype=jnp.bfloat16):
    return jax.ShapeDtypeStruct(dims, dtype)


def route(move):
    lats, lons = lax.axis_size("lat"), lax.axis_size("lon")
    pairs = []
    for lat in range(lats):
        for lon in range(lons):
            to_lat, to_lon = move(lat, lon, lats, lons)
            pairs.append((lat * lons + lon, to_lat * lons + to_lon))
    return pairs


def swap(block, lat_bits, lon_bits):
    return lax.ppermute(
        block, AXES, route(lambda lat, lon, lats, lons: (lat ^ lat_bits, lon ^ lon_bits))
    )


def outer_move(lat, lon, lats, lons):
    if lat == 0 or lat == lats - 1:
        return lat, (lon + lons // 2) % lons
    return (lat - 1 if lat % 2 == 0 else lat + 1), lon


def along_move(lat, lon, lats, lons):
    return lat, (lon + 2 if lon % 2 else lon - 2) % lons


def across_move(lat, lon, lats, lons):
    return lat, (lon + 1 if lon % 2 else lon - 1) % lons


def lane_of(value):
    return lax.broadcasted_iota(jnp.int32, value.shape, 1)


def turned(value, lanes):
    return pltpu.roll(value, lanes, 1)


def put(refs, odd, at, low, high):
    wide = low.shape[1]
    low, high = low.astype(jnp.bfloat16), high.astype(jnp.bfloat16)
    refs[0][:, at : at + wide] = jnp.where(odd == 1, high, low)
    refs[1][:, at : at + wide] = jnp.where(odd == 1, low, high)


def put_main(refs, odd, at, value, main):
    put(refs, odd, at, value[:, :main], value[:, main : 2 * main])


def split_of(value, main):
    return value[:, 2 * main : 2 * main + LANES].astype(jnp.float32)


def put_pair(refs, odd, at, first, second, main):
    put_main(refs, odd, at, first, main)
    put_main(refs, odd, at + main, second, main)
    first, second = split_of(first, main), split_of(second, main)
    front = lane_of(first) < HALF
    low = jnp.where(front, first, turned(second, HALF))
    high = jnp.where(front, turned(first, HALF), second)
    put(refs, odd, at + 2 * main, low, high)


def spare_of(tile, values, main, start):
    lane = lane_of(tile)
    for at, value in enumerate(values):
        last = value[:, 2 * main + LANES :].astype(jnp.float32)
        tile = jnp.where(lane == start + at, jnp.broadcast_to(last, tile.shape), tile)
    return tile


def weight_kernel(main, w_ref, own_ref, pair_ref):
    odd = lax.axis_index("lon") % 2
    refs = own_ref, pair_ref
    bases = w_ref.shape[0]
    values = [w_ref[k] for k in range(bases)]
    for k in range(0, bases - 1, 2):
        put_pair(refs, odd, k // 2 * (2 * main + LANES), values[k], values[k + 1], main)
    at = bases // 2 * (2 * main + LANES)
    put_main(refs, odd, at, values[-1], main)
    tile = split_of(values[-1], main)
    front = lane_of(tile) < HALF
    low, high = jnp.where(front, tile, 0.0), jnp.where(front, turned(tile, HALF), 0.0)
    put(refs, odd, at + main, low, spare_of(high, values, main, HALF))


def edge_kernel(x_ref, outer_ref, held_ref):
    radius = outer_ref.shape[0]
    lower = lax.axis_index("lat") % 2
    outer_ref[...] = jnp.where(lower == 1, x_ref[-radius:], x_ref[:radius])
    held_ref[...] = x_ref[...]


def start_kernel(main, w_ref, x_ref, own_ref, pair_ref, outer_ref, held_ref):
    weight_kernel(main, w_ref, own_ref, pair_ref)
    edge_kernel(x_ref, outer_ref, held_ref)


def strip_kernel(main, x_ref, outer_ref, mine_ref, other_ref, rows_ref):
    lat, odd = lax.axis_index("lat"), lax.axis_index("lon") % 2
    pole = (lat == 0) | (lat == lax.axis_size("lat") - 1)
    radius, rows = outer_ref.shape[0], x_ref.shape[0]
    rows_ref[pl.ds((1 - lat % 2) * radius, rows)] = x_ref[...]
    for r in range(radius):
        rows_ref[lat % 2 * rows + r] = outer_ref[jnp.where(pole, radius - 1 - r, r)]
    refs = mine_ref, other_ref
    count = rows_ref.shape[0]
    values = [rows_ref[r] for r in range(count)]
    for r in range(count // 2):
        at = r * (2 * main + LANES)
        put_pair(refs, odd, at, values[r], values[r + count // 2], main)
    none = jnp.zeros((x_ref.shape[1], LANES), jnp.float32)
    put(refs, odd, count // 2 * (2 * main + LANES), none, spare_of(none, values, main, 0))


def join_kernel(mine_ref, other_ref, out_ref):
    odd = lax.axis_index("lon") % 2
    share = mine_ref.shape[0]
    low, high = mine_ref[...], other_ref[...]
    out_ref[:share] = jnp.where(odd == 1, high, low)
    out_ref[share:] = jnp.where(odd == 1, low, high)


def copy_kernel(source_ref, out_ref):
    out_ref[...] = source_ref[...]


def stack_kernel(*refs):
    for at, ref in enumerate(refs[:-1]):
        refs[-1][at] = ref[...]


def band_kernel(reach, f_ref, w_ref, band_ref, row_ref):
    bases, span, rows, taps = f_ref.shape
    columns = band_ref.shape[1] // (2 * bases)
    pitch = columns + taps - 1
    wide = band_ref.shape[2]
    offset = jnp.abs(lax.broadcasted_iota(jnp.int32, (rows, taps), 1) - reach)
    row_ref[...] = jnp.zeros_like(row_ref)
    for d in range(span):
        inside = offset <= w_ref[:, d : d + 1]
        for k in range(bases):
            tap = jnp.where(inside, f_ref[k, d].astype(jnp.float32), 0.0)
            row_ref[k, :, d * pitch : d * pitch + taps] = tap

    def one_pair(pair, _):
        for e in range(2):
            for k in range(bases):
                same = jnp.broadcast_to(row_ref[k, pl.ds(2 * pair + e, 1), :], (columns, wide))
                band = pltpu.roll(same, e * pitch, 1, stride=1, stride_axis=0)
                at = (e * bases + k) * columns
                band_ref[pair, at : at + columns, :] = band.astype(jnp.bfloat16)
        return 0

    lax.fori_loop(0, rows // 2, one_pair, 0)


def unpack(source_ref, slab_ref, slot, main):
    count = slab_ref.shape[0]
    wide = 2 * main + LANES
    spare = source_ref[:, count // 2 * wide :].astype(jnp.float32)
    lane = lane_of(spare)
    for r in range(count // 2):
        tile = source_ref[:, r * wide + 2 * main : (r + 1) * wide].astype(jnp.float32)
        for row, third in ((r, tile), (r + count // 2, turned(tile, HALF))):
            at = r * wide + (main if row > r else 0)
            slab_ref[row, slot, :, :main] = source_ref[:, at : at + main]
            last = turned(spare, (HALF - row) % LANES)
            third = jnp.where(lane == HALF, last, third)
            slab_ref[row, slot, :, main:] = third.astype(jnp.bfloat16)


def slab_kernel(mine_ref, pair_ref, along_ref, across_ref, slab_ref, inner_ref):
    odd = lax.axis_index("lon") % 2
    main = slab_ref.shape[3] - LANES
    unpack(mine_ref, slab_ref, 1 + odd, main)
    unpack(pair_ref, slab_ref, 2 - odd, main)
    unpack(along_ref, slab_ref, 3 * (1 - odd), main)
    unpack(across_ref, slab_ref, 3 * odd, main)
    radius = inner_ref.shape[0]
    start = (1 - lax.axis_index("lat") % 2) * (slab_ref.shape[0] - radius)
    inner_ref[...] = slab_ref[pl.ds(start, radius)]


def feature_kernel(span, band_ref, rows_ref, inner_ref, out_ref, slab_ref):
    lower = lax.axis_index("lat") % 2
    held, radius = rows_ref.shape[0], inner_ref.shape[0]
    slab_ref[pl.ds(lower * radius, held)] = rows_ref[...]
    slab_ref[pl.ds((1 - lower) * held, radius)] = inner_ref[...]
    strips, rows, columns, _ = out_ref.shape
    half = slab_ref.shape[3]
    main = half - LANES
    bases = band_ref.shape[1] // (2 * columns)
    depth = (span + 1) * 3 * columns
    wide = 2 * main + LANES

    def one_pair(pair, _):
        band = band_ref[pair][:, :depth]
        source = [
            slab_ref[pl.ds(2 * pair, span + 1), strip : strip + 3].reshape(depth, half)
            for strip in range(strips)
        ]
        summed = jnp.dot(
            band, jnp.concatenate(source, axis=1), preferred_element_type=jnp.float32
        )
        for e in range(2):
            for strip in range(strips):

                def save(at, value):
                    out_ref[strip, 2 * pair + e, :, at : at + value.shape[1]] = value.astype(
                        jnp.bfloat16
                    )

                parts = []
                for k in range(bases):
                    at = (e * bases + k) * columns
                    parts.append(summed[at : at + columns, strip * half : (strip + 1) * half])
                lane = lane_of(parts[0][:, main:])
                for k, part in enumerate(parts):
                    save(k // 2 * wide + k % 2 * main, part[:, :main])
                for k in range(0, bases - 1, 2):
                    second = turned(parts[k + 1][:, main:], HALF)
                    save(k // 2 * wide + 2 * main, jnp.where(lane < HALF, parts[k][:, main:], second))
                tile = parts[-1][:, main:]
                for k in range(bases):
                    tile = jnp.where(lane == HALF + k, turned(parts[k][:, main:], k), tile)
                save(bases // 2 * wide + main, tile)
        return 0

    lax.fori_loop(0, rows // 2, one_pair, 0)


def product(feature_ref, strip, weight):
    return lax.dot_general(
        feature_ref[strip], weight, (((1,), (1,)), ((), ())), preferred_element_type=jnp.float32
    )


def partner_mix_kernel(sources, feature_ref, *refs):
    piece_refs = refs[: len(sources)]
    send_ref, weight_ref = refs[len(sources) :]
    lat, lon = lax.axis_index("lat"), lax.axis_index("lon")
    masks = lax.axis_size("lon") // 2
    if sum(len(held) for _, _, held in sources) < weight_ref.shape[0]:
        weight_ref[...] = jnp.zeros_like(weight_ref)
    for (core, low, held), ref in zip(sources, piece_refs):
        row = 2 * ((lat // 2) ^ low) + (lat % 2 ^ core)
        for at, mask in enumerate(held):
            weight_ref[row * masks + ((lon // 2) ^ mask)] = ref[at]
    weight = weight_ref[...].reshape(send_ref.shape[1], weight_ref.shape[2])
    send_ref[...] = product(feature_ref, 1 - lon % 2, weight).astype(send_ref.dtype)


def own_mix_kernel(feature_ref, weight_ref, keep_ref):
    weight = weight_ref[...].reshape(keep_ref.shape[1], weight_ref.shape[2])
    keep_ref[...] = product(feature_ref, lax.axis_index("lon") % 2, weight)


def rest_kernel(own, feature_ref, own_ref, crossed_ref, sum_ref):
    odd = lax.axis_index("lon") % 2
    weight = jnp.concatenate([own_ref[0], crossed_ref[0]], axis=0)
    count = sum_ref.shape[0]
    total = product(feature_ref, odd if own else 1 - odd, weight)
    sum_ref[...] = jnp.concatenate([total[:count], total[count:]], axis=1).astype(sum_ref.dtype)


def grown(total):
    return 0.5 * total * (1.0 + lax.erf(total * 0.5**0.5))


def main_kernel(keep_ref, got_ref, bias_ref, out_ref):
    total = keep_ref[...] + got_ref[...].astype(jnp.float32) + bias_ref[...]
    out_ref[...] = grown(total).astype(out_ref.dtype)


def finish_kernel(last, block, main_ref, keep_ref, got_ref, bias_ref, out_ref):
    lat, lon = lax.axis_index("lat"), lax.axis_index("lon")
    out_ref[...] = main_ref[...]
    rest = keep_ref[...] + got_ref[...].astype(jnp.float32)
    count = rest.shape[0]
    lane = lane_of(rest)
    start = ((lon // 2) ^ last) * block
    inside = (lane >= start) & (lane < start + block)
    spots = []
    for crossed in range(2):
        tile = (1 - lat // 2) * 2 + (lat % 2 ^ crossed)
        at = pl.ds(pl.multiple_of(tile * LANES, LANES), LANES)
        spots += [(at, part, part * (2 * block) + crossed * block) for part in range(2)]
    bias = jnp.zeros((8, LANES), jnp.float32)
    narrow = lane_of(bias)
    for at, _, held in spots:
        moved = jnp.broadcast_to(bias_ref[:, at], bias.shape)
        moved = pltpu.roll(moved, lax.rem(held - start + LANES, LANES), 1)
        bias = jnp.where((narrow >= held) & (narrow < held + block), moved, bias)
    value = grown(rest + bias[:1])
    for at, part, held in spots:
        rows = slice(part * count, (part + 1) * count)
        moved = pltpu.roll(value, lax.rem(start - held + LANES, LANES), 1)
        merged = jnp.where(inside, moved, main_ref[rows, at].astype(jnp.float32))
        out_ref[rows, at] = merged.astype(out_ref.dtype)


def body(latent, filters, widths, mix_weight, mix_bias):
    lats, lons = lax.axis_size("lat"), lax.axis_size("lon")
    rows, columns, channels = latent.shape
    bases, _, span, taps = filters.shape
    radius, reach = span // 2, taps // 2
    assert reach == columns and rows % 2 == lats % 2 == lons % 2 == 0
    main = channels // (2 * LANES) * LANES
    assert channels == 2 * main + LANES + 1 and bases % 2 == 1
    assert bases <= HALF and rows + 2 * radius <= LANES
    half, packed = main + LANES, 2 * main + LANES
    out_columns, share = mix_bias.shape[0], mix_weight.shape[2]
    depth = bases // 2 * packed + half

    edge, halves = shape((radius, columns, channels)), shape((share, depth))
    weights = jnp.transpose(mix_weight, (0, 2, 1))
    own_weight, pair_weight = call(
        functools.partial(weight_kernel, main), (halves, halves), [], weights
    )
    outer, held_latent = call(edge_kernel, (edge, shape(latent.shape)), [], latent)
    from_outer = lax.ppermute(outer, AXES, route(outer_move))
    got_weight = swap(pair_weight, 0, 1)
    block = shape((2 * share, depth))
    first = call(join_kernel, block, [], own_weight, got_weight)

    lon_masks, lat_masks = lons // 2, lats // 2
    steps = [1 << at for at in range(lat_masks.bit_length() - 1)]
    blocks = {(0, 0): first}
    bit = lon_masks // 2
    while bit:
        for low, mask in list(blocks):
            blocks[low, mask ^ bit] = swap(blocks[low, mask], 0, 2 * bit)
        bit //= 2
    order = [mask for _, mask in blocks]
    last = order[-1]
    count = rows + radius
    strip = shape((columns, count // 2 * packed + LANES))

    def cross(masks):
        for bit in steps:
            for low in range(bit):
                for mask in masks:
                    blocks[low ^ bit, mask] = swap(blocks[low, mask], 2 * bit, 0)

    cross(order[:1])
    mine, other = call(
        functools.partial(strip_kernel, main),
        (strip, strip),
        [pltpu.VMEM((count, columns, channels), jnp.bfloat16)],
        held_latent,
        from_outer,
    )
    for mask in order[1:-1]:
        blocks[0, mask] = call(copy_kernel, block, [], blocks[0, mask], after=(mine,))
    cross(order[1:-1])
    across = lax.ppermute(other, AXES, route(across_move))
    along = lax.ppermute(mine, AXES, route(along_move))
    pair_strip = swap(other, 0, 1)
    deep = -(-(span + 1) * 3 * columns // LANES) * LANES
    band = call(
        functools.partial(band_kernel, reach),
        shape((rows // 2, 2 * bases * columns, deep)),
        [pltpu.VMEM((bases, rows, deep), jnp.float32)],
        jnp.transpose(filters, (0, 2, 1, 3)),
        widths,
        after=(pair_strip,),
    )
    slab, inner = call(
        slab_kernel,
        (shape((count, 4, columns, half)), shape((radius, 4, columns, half))),
        [],
        mine,
        pair_strip,
        along,
        across,
    )
    from_inner = swap(inner, 1, 0)

    features = call(
        functools.partial(feature_kernel, span),
        shape((2, rows, columns, depth)),
        [pltpu.VMEM((rows + 2 * radius, 4, columns, half), jnp.bfloat16)],
        band,
        slab,
        from_inner,
    )
    features = features.reshape(2, rows * columns, depth)
    met = [value for key, value in blocks.items() if key != (0, last)]
    blocks[0, last] = call(
        copy_kernel, block, [], blocks[0, last], after=(*met, features)
    )
    cross(order[-1:])
    points = rows * columns

    def stacked(low, held, after):
        piece = call(
            stack_kernel,
            shape((len(held),) + block.shape),
            [],
            *[blocks[low, mask] for mask in held],
            after=after,
        )
        return [piece, swap(piece, 1, 0)]

    apart = lat_masks == 2 and 8 * share == LANES == lon_masks * 2 * share and points % 2 == 0
    sources, pieces = [], []
    for low in range(lat_masks):
        held = order[:-1] if low and apart else order
        sources += [(core, low, held) for core in range(2)]
        pieces += stacked(low, held, (blocks[0, last],) if low == 0 else (blocks[0, last],))
    send, weight = call(
        functools.partial(partner_mix_kernel, sources),
        (shape((points, out_columns)), shape((lats * lon_masks,) + block.shape)),
        [],
        features,
        *pieces,
    )
    got = swap(send, 0, 1)
    sums = shape((points, out_columns), jnp.float32)
    if not apart:
        keep = call(own_mix_kernel, sums, [], features, weight)
        total = (keep + got.astype(jnp.float32)).reshape(rows, columns, out_columns) + mix_bias
        return jax.nn.gelu(total, approximate=False).astype(jnp.bfloat16)
    rest, pieces = (points // 2, LANES), stacked(1, order[-1:], (send,))
    rest_send = call(
        functools.partial(rest_kernel, False), shape(rest), [], features, *pieces
    )
    rest_got = swap(rest_send, 0, 1)
    keep = call(own_mix_kernel, sums, [], features, weight, after=(rest_send,))
    rest_keep = call(
        functools.partial(rest_kernel, True),
        shape(rest, jnp.float32),
        [],
        features,
        *pieces,
        after=(rest_send,),
    )
    done = call(
        main_kernel, shape((points, out_columns)), [], keep, got, mix_bias[None]
    )
    out = call(
        functools.partial(finish_kernel, last, 2 * share),
        shape((points, out_columns)),
        [],
        done,
        rest_keep,
        rest_got,
        mix_bias[None],
    )
    return out.reshape(rows, columns, out_columns)


def solution(mesh):
    placed = (
        P("lat", "lon", None),
        P(None, "lat", None, None),
        P("lat", None),
        P(None, None, ("lat", "lon")),
        P(),
    )
    return jax.shard_map(
        body, mesh=mesh, in_specs=placed, out_specs=P("lat", "lon", None), check_vma=False
    )
```
